256 devices in a mesh: context: 64 (over y, z, core), tensor: 4 (over x).
Axes of the slice: x: 4, y: 4, z: 8, core: 2. Of those that a mesh axis runs over, the one named last changes fastest.
Arguments:
- layer_input: bfloat16 [32768, 1024], P('context', 'tensor'), may hold values from -16 to 16
- value_proj: bfloat16 [1024, 2048], P(None, 'tensor'), may hold values from -0.1875 to 0.1875
- conv_taps: float32 [4, 2048], P(None, 'tensor'), may hold values from -3 to 3
- conv_pre: bfloat16 [32768, 2048], P('context', 'tensor'), may hold values from -6 to 6
- state_in: bfloat16 [32768, 128], P('context'), may hold values from -6 to 6
- state_out: bfloat16 [32768, 128], P('context'), may hold values from -0.5 to 0.5
- step_size: float32 [32, 32768], P('tensor', 'context'), may hold values from 0 to 1
- log_decay: float32 [32, 32768], P('tensor', 'context'), may hold values from -2 to 0
- skip_gain: float32 [32], P('tensor'), may hold values from 0.5 to 2
- grad_out: bfloat16 [32768, 2048], P('context', 'tensor'), may hold values from -6 to 6
Outputs:
- grad_input: bfloat16 [32768, 1024], P('context', 'tensor')
- grad_value_proj: float32 [1024, 2048], P('context', 'tensor')
The draws below stay inside these ranges and needn't reach their ends.
All inputs are finite; a program needn't handle non-finite values.
Results may differ from the reference program's by a relative error of at most 0.0059.
Values may be sent and summed in bfloat16 or wider, within the bound.
A program may use at most 64 MiB of HBM per device.

```python
import math
import jax
import jax.numpy as jnp
from jax import lax

D = 1024
HEADS = 32
HEAD_DIM = 64
STATE = 128
CONV = 4
BLOCK = 256
TOK_DEV = 512
INNER = 2048
TOKEN_SPAN = 32768


def head_rates(key, fast_share, chain_share):
    chooser_key, chain_key, device_key, fast_key = jax.random.split(key, 4)
    chooser = jax.random.uniform(chooser_key, (HEADS,))
    chain_rate = jnp.exp(jax.random.uniform(chain_key, (HEADS,), minval=math.log(0.15), maxval=math.log(0.8))) * 2.3 / TOKEN_SPAN
    device_rate = jnp.exp(jax.random.uniform(device_key, (HEADS,), minval=math.log(0.25), maxval=0.0)) * 2.3 / TOK_DEV
    fast_rate = 2.3 / jnp.exp(jax.random.uniform(fast_key, (HEADS,), minval=math.log(30.0), maxval=math.log(50.0)))
    slow_rate = jnp.where(chooser < fast_share + chain_share, chain_rate, device_rate)
    return jnp.where(chooser < fast_share, fast_rate, slow_rate)


def draw_log_decay(key, part):
    rates = head_rates(key, 0.35, 0.45)
    key = jax.random.fold_in(key, 11)
    angle_seed_handle, coarse_seed_handle, spike_seed_handle, magnitude_seed_handle = jax.random.split(key, 4)
    places = jnp.arange(TOKEN_SPAN, dtype=jnp.float32)
    phase = jax.random.uniform(angle_seed_handle, (), minval=0.0, maxval=2.0 * math.pi)
    swing = jnp.exp(0.8 * jnp.sin(2.0 * math.pi * 3.0 * places / TOKEN_SPAN + phase))
    rough = jnp.exp(jax.random.uniform(coarse_seed_handle, (HEADS, TOKEN_SPAN), minval=math.log(0.5), maxval=math.log(2.0)))
    placement_indices = jax.random.randint(spike_seed_handle, (2,), 0, TOKEN_SPAN)
    struck = jnp.any(jnp.arange(TOKEN_SPAN)[None, :] == placement_indices[:, None], axis=0)
    amount = jax.random.uniform(magnitude_seed_handle, (HEADS, TOKEN_SPAN), minval=0.22, maxval=0.51)
    return -(rates[:, None] * swing[None, :] * rough) - jnp.where(struck[None, :], amount, 0.0)


def draw_step_size(key, part):
    rates = head_rates(key, 0.35, 0.45)
    key = jax.random.fold_in(key, 12)
    jitter = jax.random.uniform(key, (HEADS, TOKEN_SPAN), minval=0.5, maxval=1.5)
    return jnp.sqrt(rates)[:, None] * jitter


def strengthened(drawn, rng, source, target, shards_of, factor):
    def block_of(dim):
        return (jnp.arange(drawn.shape[dim]) // (drawn.shape[dim] // shards_of)).reshape((-1,) + (1,) * (drawn.ndim - 1 - dim))

    first = jax.random.permutation(rng, shards_of)[block_of(target)]
    other_side = (block_of(target) + shards_of // 2) % shards_of
    return jnp.where((block_of(source) == first) | (block_of(source) == other_side), factor * drawn, drawn)


def block_levels(own_key, extent, cuts, least, largest):
    factor_of = 1.0
    for axis_at, parts in cuts:
        steps = jax.random.uniform(jax.random.fold_in(jax.random.fold_in(own_key, 6), axis_at), (parts,), jnp.float32, least / len(cuts), largest / len(cuts))
        factor_of = factor_of * jnp.repeat(jnp.exp(steps), extent[axis_at] // parts).reshape((-1,) + (1,) * (len(extent) - 1 - axis_at))
    return factor_of


def gaussian(key, dims, scale, reach, cuts=(), kind=jnp.bfloat16):
    drawn = scale * jax.random.normal(key, dims, jnp.float32)
    if cuts:
        drawn = drawn * block_levels(key, dims, cuts, -0.22, 0.18)
    return jnp.clip(drawn, -reach, reach).astype(kind)


def heavy_noise(own_key, dims, width, bound, shards, heavy, kind=jnp.bfloat16):
    array = width * jax.random.normal(own_key, dims, jnp.float32)
    if shards:
        array = array * block_levels(own_key, dims, shards, -0.22, 0.18)
    return jnp.clip(strengthened(array, jax.random.fold_in(own_key, 3), *heavy), -bound, bound).astype(kind)


def setup_inputs(seed: int = 0) -> dict:
    key_of = jax.random.split(jax.random.key(seed), 11)
    layer_input = heavy_noise(key_of[0], (TOKEN_SPAN, D), 1.0, 16.0, ((0, 64), (1, 4)), (0, 1, 64, 4.0))
    value_proj = gaussian(key_of[1], (D, INNER), D ** -0.5, 0.1875, ((1, 4),))
    conv_taps = gaussian(key_of[2], (CONV, INNER), CONV ** -0.5, 3.0, ((1, 4),), jnp.float32)
    conv_pre = gaussian(key_of[3], (TOKEN_SPAN, INNER), 1.0, 6.0, ((0, 64), (1, 4)))
    state_in = gaussian(key_of[4], (TOKEN_SPAN, STATE), 1.0, 6.0, ((0, 64),))
    state_out = gaussian(key_of[5], (TOKEN_SPAN, STATE), STATE ** -0.5, 0.5, ((0, 64),))
    step_size = draw_step_size(jax.random.fold_in(key_of[10], 71), 0)
    log_decay = draw_log_decay(jax.random.fold_in(key_of[10], 71), 0)
    skip_gain = jnp.clip(0.5 + 1.5 * jax.random.uniform(key_of[8], (HEADS,), jnp.float32) ** block_levels(key_of[8], (HEADS,), ((0, 4),), -0.2, 0.2), 0.5, 2.0)
    grad_out = gaussian(key_of[9], (TOKEN_SPAN, INNER), 1.0, 6.0, ((0, 64), (1, 4)))
    return dict(layer_input=layer_input, value_proj=value_proj, conv_taps=conv_taps, conv_pre=conv_pre, state_in=state_in, state_out=state_out, step_size=step_size, log_decay=log_decay, skip_gain=skip_gain, grad_out=grad_out)


precise = lax.Precision.HIGHEST

def silu_slope(values):
    sigmoid_value = jax.nn.sigmoid(values)
    return sigmoid_value * (1.0 + values * (1.0 - sigmoid_value))

def block_grads(carried, input_blk, output_blk, grad_blk, step_blk, decay_blk, skip_gain):
    running_total = jnp.cumsum(decay_blk, axis=1)
    closing = running_total[:, -1:]
    length = input_blk.shape[0]
    scores = jnp.dot(input_blk, output_blk.T, preferred_element_type=jnp.float32)
    spread = running_total[:, None, :] - running_total[:, :, None]
    upper_mask = jnp.arange(length)[None, :] >= jnp.arange(length)[:, None]
    damping = jnp.where(upper_mask[None], jnp.exp(jnp.minimum(spread, 0.0)), 0.0)
    weights = (scores[None] * damping).astype(jnp.bfloat16)
    grad_float = grad_blk.astype(jnp.float32)
    within = jnp.einsum('hts,shp->thp', weights.astype(jnp.float32), grad_float, precision=precise)
    carried_low = lax.optimization_barrier(carried.astype(jnp.bfloat16)).astype(jnp.float32)
    beyond = jnp.einsum('hpn,tn->thp', carried_low, input_blk.astype(jnp.float32), precision=precise)
    beyond = beyond * jnp.exp(closing - running_total).T[:, :, None]
    grad_x = step_blk.T[:, :, None] * (within + beyond) + skip_gain[None, :, None] * grad_float
    weighted = (grad_float * jnp.exp(running_total).T[:, :, None]).astype(jnp.bfloat16)
    weighted = lax.optimization_barrier(weighted).astype(jnp.float32)
    block_state = jnp.einsum('shp,sn->hpn', weighted, output_blk.astype(jnp.float32), precision=precise)
    return (grad_x, jnp.exp(closing)[:, :, None] * carried + block_state)

def reference(layer_input, value_proj, conv_taps, conv_pre, state_in, state_out, step_size, log_decay, skip_gain, grad_out):
    block_count = TOKEN_SPAN // BLOCK
    block_parts = (state_in.reshape(block_count, BLOCK, STATE), state_out.reshape(block_count, BLOCK, STATE), grad_out.reshape(block_count, BLOCK, HEADS, HEAD_DIM), conv_pre.reshape(block_count, BLOCK, INNER), step_size.reshape(HEADS, block_count, BLOCK).transpose(1, 0, 2), log_decay.reshape(HEADS, block_count, BLOCK).transpose(1, 0, 2))

    def block_step(carried, pieces):
        grad_x, carried = block_grads(carried, pieces[0], pieces[1], pieces[2], pieces[4], pieces[5], skip_gain)
        slope = silu_slope(pieces[3].astype(jnp.float32))
        grad_conv = (grad_x.reshape(BLOCK, INNER) * slope).astype(jnp.bfloat16)
        return (carried, grad_conv)
    empty_state = jnp.zeros((HEADS, HEAD_DIM, STATE), jnp.float32)
    grad_conv = lax.scan(block_step, empty_state, block_parts, reverse=True)[1].reshape(TOKEN_SPAN, INNER)
    extended = jnp.concatenate([grad_conv.astype(jnp.float32), jnp.zeros((CONV - 1, INNER), jnp.float32)], axis=0)
    summed = jnp.zeros((TOKEN_SPAN, INNER), jnp.float32)
    for offset in range(CONV):
        start_row = CONV - 1 - offset
        summed = summed + conv_taps[offset][None, :] * extended[start_row:start_row + TOKEN_SPAN]
    grad_proj = summed.astype(jnp.bfloat16)
    grad_input = jnp.dot(grad_proj, value_proj.T, preferred_element_type=jnp.float32).astype(jnp.bfloat16)
    grad_value_proj = jnp.dot(layer_input.T, grad_proj, preferred_element_type=jnp.float32) * (1.0 / math.sqrt(TOKEN_SPAN))
    return (grad_input, grad_value_proj)
```

```python
import functools
import math

import jax
import jax.numpy as jnp
from jax import lax
from jax.experimental import pallas as pl
from jax.experimental.pallas import tpu as pltpu
from jax.sharding import PartitionSpec as P

MESH = pl.DeviceIdType.MESH
F32, BF16 = jnp.float32, jnp.bfloat16
HIGH = lax.Precision.HIGHEST

NX, NY, NZ, NC = 4, 4, 8, 2
NROW = NZ * NC
NCTX = NY * NROW
ROWS, CH, STATE, BLOCK, HEADS, HD = 512, 512, 128, 256, 8, 64
FEAT = 256
Q, QW = 2, 256
TILE, NT = 128, 4


def dot(a, b, dims, precision=None):
    return lax.dot_general(a, b, (dims, ((), ())), precision=precision, preferred_element_type=F32)


def remote(src, dst, send, recv, ctx, ten):
    return pltpu.make_async_remote_copy(
        src_ref=src, dst_ref=dst, send_sem=send, recv_sem=recv,
        device_id=(ctx, ten), device_id_type=MESH,
    )


def kernel(
    lay_h, vp_h, taps_h, pre_h, sin_h, sout_h, step_h, ld_h, skip_h, go_h,
    gi_ref, gv_ref,
    lay, vp, taps, pre, sin, sout, step, ld, skip, go,
    cum, a_ref, b_ref, gc, gp, bs1, clos, lt,
    s_send, s_recv, d_send, d_recv, rsuf, lsuf, y_send, y_recv, c_send, carry,
    p_send, x_recv, x_own,
    w_send, w_recv, w_own, v_send, v_recv, u_own, u_send, u_recv,
    in_sem, lay_ss, lay_rs, s_ss, s_rs, d_ss, d_rs, y_ss, y_rs, c_ss, c_rs, h_ss, h_rs,
    x_ss, x_rs, w_ss, w_rs, v_ss, v_rs, u_ss, u_rs,
):
    c = lax.axis_index("context")
    t = lax.axis_index("tensor")
    core = lax.rem(c, NC)
    z = lax.rem(c // NC, NZ)
    y = c // NROW
    i = lax.rem(c, NROW)
    row0 = y * NROW
    nxt, prv = lax.rem(c + 1, NCTX), lax.rem(c + NCTX - 1, NCTX)

    barrier = pltpu.get_barrier_semaphore()

    def greet(ctx, ten):
        pl.semaphore_signal(barrier, inc=1, device_id=(ctx, ten), device_id_type=MESH)

    def greet_row(k, _):
        greet(row0 + lax.rem(i + k, NROW), t)
        return 0

    lax.fori_loop(1, NROW, greet_row, 0)
    for k in range(1, NY):
        greet(lax.rem(c + k * NROW, NCTX), t)
    for k in range(1, NX):
        greet(c, lax.rem(t + k, NX))
    greet(nxt, t)
    greet(prv, t)

    loads = {}
    for n, (name, src, dst) in enumerate((
        ("ld", ld_h, ld), ("go", go_h, go), ("sout", sout_h, sout), ("sin", sin_h, sin),
        ("step", step_h, step), ("skip", skip_h, skip), ("pre", pre_h, pre), ("taps", taps_h, taps),
        ("vp", vp_h, vp), ("lay", lay_h, lay.at[t]),
    )):
        loads[name] = pltpu.make_async_copy(src, dst, in_sem.at[n])
        loads[name].start()

    ri = lax.broadcasted_iota(jnp.int32, (BLOCK, BLOCK), 0)
    ci = lax.broadcasted_iota(jnp.int32, (BLOCK, BLOCK), 1)
    upto = (ri <= ci).astype(F32)
    hi = lax.broadcasted_iota(jnp.int32, (HEADS, CH), 0)
    li = lax.broadcasted_iota(jnp.int32, (HEADS, CH), 1)
    onehot = (li // HD == hi).astype(F32)
    loads["ld"].wait()
    for k in range(2):
        cum[:, k * BLOCK:(k + 1) * BLOCK] = dot(ld[:, k * BLOCK:(k + 1) * BLOCK], upto, ((1,), (0,)), HIGH)
    for k in range(2):
        b_ref[k * BLOCK:(k + 1) * BLOCK, :] = dot(cum[:, k * BLOCK:(k + 1) * BLOCK], onehot, ((0,), (0,)), HIGH)
    clos0 = b_ref[BLOCK - 1:BLOCK, :]
    clos1 = b_ref[2 * BLOCK - 1:2 * BLOCK, :]
    clos[0:1, :] = clos0
    clos[1:2, :] = clos1
    for k in range(NC):
        d_send[k] = (clos0 + clos1)[:, k * 256:(k + 1) * 256]

    pl.semaphore_wait(barrier, NROW - 1 + NY - 1 + NX - 1 + 2)

    def d_copy(k):
        j = lax.rem(i + k, NROW)
        return remote(d_send.at[lax.rem(j, NC)], d_recv.at[i], d_ss.at[j], d_rs.at[i], row0 + j, t)

    def start_d(k, _):
        d_copy(k).start()
        return 0

    lax.fori_loop(1, NROW, start_d, 0)
    d_recv[i] = d_send[core]

    for k in (1, 3, 2):
        tt = lax.rem(t + k, NX)
        remote(lay_h, lay.at[t], lay_ss.at[tt], lay_rs.at[t], c, tt).start()

    loads["go"].wait()
    loads["sout"].wait()
    state = None
    for k in range(2):
        w = (go[k * BLOCK:(k + 1) * BLOCK, :].astype(F32) * jnp.exp(b_ref[k * BLOCK:(k + 1) * BLOCK, :])).astype(BF16)
        bs = dot(sout[k * BLOCK:(k + 1) * BLOCK, :], w, ((0,), (0,)))
        if k == 0:
            state = bs
        else:
            bs1[...] = bs
            state = state + jnp.exp(clos0) * bs
    state = state.astype(BF16)
    for k in range(NC):
        s_send[k] = state[:, k * 256:(k + 1) * 256]

    def s_copy(k):
        j = lax.rem(i + k, NROW)
        rows = pl.ds(pl.multiple_of((j // NC) * 16, 16), 16)
        return remote(s_send.at[lax.rem(j, NC), rows], s_recv.at[i], s_ss.at[j], s_rs.at[i], row0 + j, t)

    def start_s(k, _):
        s_copy(k).start()
        return 0

    lax.fori_loop(1, NROW, start_s, 0)
    s_recv[i] = s_send[core, pl.ds(pl.multiple_of(z * 16, 16), 16), :]

    for name in ("sin", "step", "skip", "pre"):
        loads[name].wait()
    skip_e = dot(skip[...], onehot, ((1,), (0,)), HIGH)

    def within(k):
        r0 = k * BLOCK
        rows = slice(r0, r0 + BLOCK)
        scores = dot(sin[rows, :], sout[rows, :], ((1,), (1,)))
        scores = jnp.where(ci >= ri, scores, 0.0)
        low = lax.broadcasted_iota(jnp.int32, (BLOCK, 128), 1) < HD
        cum_t = cum[:, rows].T
        for pair in range(HEADS // 2):
            lanes = slice(pair * 128, pair * 128 + 128)
            g = go[rows, lanes]
            parts = []
            for h in (2 * pair, 2 * pair + 1):
                spread = cum[h:h + 1, rows] - cum_t[:, h:h + 1]
                weights = (scores * jnp.exp(jnp.minimum(spread, 0.0))).astype(BF16)
                parts.append(dot(weights, g, ((1,), (0,))))
            a_ref[rows, lanes] = jnp.where(low, parts[0], parts[1])

    within(0)

    def d_wait(k, _):
        j = lax.rem(i + k, NROW)
        remote(d_send.at[0], d_recv.at[j], d_ss.at[j], d_rs.at[j], c, t).wait_recv()
        return 0

    def s_wait(k, _):
        j = lax.rem(i + k, NROW)
        remote(s_send.at[0, pl.ds(0, 16)], s_recv.at[j], s_ss.at[j], s_rs.at[j], c, t).wait_recv()
        return 0

    lax.fori_loop(1, NROW, d_wait, 0)
    lax.fori_loop(1, NROW, s_wait, 0)

    def scan(k, carried):
        r, l = carried
        j = NROW - 1 - k
        rsuf[j] = r
        lsuf[j] = l
        d = d_recv[j]
        return (s_recv[j].astype(F32) + jnp.exp(d) * r, l + d)

    total, span = lax.fori_loop(0, NROW, scan, (jnp.zeros((16, 256), F32), jnp.zeros((1, 256), F32)))
    y_send[0:16, :] = total
    y_send[16:24, :] = jnp.broadcast_to(span, (8, 256))
    for k in range(1, NY):
        yy = lax.rem(y + k, NY)
        remote(y_send, y_recv.at[y], y_ss.at[yy], y_rs.at[y], lax.rem(c + k * NROW, NCTX), t).start()
    y_recv[y] = y_send[...]

    within(1)

    for k in range(1, NY):
        yy = lax.rem(y + k, NY)
        remote(y_send, y_recv.at[yy], y_ss.at[yy], y_rs.at[yy], c, t).wait_recv()
    coming = jnp.zeros((16, 256), F32)
    for yy in range(NY - 1, 0, -1):
        r = y_recv[yy]
        coming = jnp.where(yy > y, r[0:16, :] + jnp.exp(r[16:17, :]) * coming, coming)

    my_rows = pl.ds(pl.multiple_of(z * 16, 16), 16)

    def c_copy(k):
        j = lax.rem(i + k, NROW)
        return remote(c_send.at[j], carry.at[core, my_rows], c_ss.at[j], c_rs.at[i], row0 + j, t)

    def start_c(k, _):
        j = lax.rem(i + k, NROW)
        c_send[j] = (rsuf[j] + jnp.exp(lsuf[j]) * coming).astype(BF16)
        c_copy(k).start()
        return 0

    lax.fori_loop(1, NROW, start_c, 0)
    carry[core, my_rows, :] = (rsuf[i] + jnp.exp(lsuf[i]) * coming).astype(BF16)

    for k in range(2):
        close = clos[k:k + 1, :]

        def factors(n, _, k=k, close=close):
            rows = pl.ds(pl.multiple_of(k * BLOCK + n * 64, 64), 64)
            v = pre[rows, :].astype(F32)
            sig = 1.0 / (1.0 + jnp.exp(-v))
            slope = sig * (1.0 + v * (1.0 - sig))
            step_e = dot(step_t(k * BLOCK + n * 64), onehot, ((0,), (0,)), HIGH)
            a_ref[rows, :] = (step_e * a_ref[rows, :] + skip_e * go[rows, :].astype(F32)) * slope
            b_ref[rows, :] = step_e * jnp.exp(close - b_ref[rows, :]) * slope
            return 0

        def step_t(start):
            return step[:, start:start + 64]

        for n in range(4):
            factors(n, 0)

    loads["lay"].wait()
    for k in range(1, NX):
        tt = lax.rem(t + k, NX)
        remote(lay_h, lay.at[tt], lay_ss.at[tt], lay_rs.at[tt], c, tt).wait_recv()

    def transposed(x, _):
        for half in range(2):
            cols = slice(half * 256, half * 256 + 256)
            tr = lay[x, cols, :].T
            for zz in range(NZ):
                for cc in range(NC):
                    f0 = (zz * NC + cc) * 16
                    lt[cc, pl.ds(pl.multiple_of(x * 128 + zz * 16, 16), 16), cols] = tr[f0:f0 + 16, :]
        return 0

    lax.fori_loop(0, NX, transposed, 0)

    def c_wait(k, _):
        j = lax.rem(i + k, NROW)
        rows = pl.ds(pl.multiple_of((j // NC) * 16, 16), 16)
        remote(c_send.at[j], carry.at[lax.rem(j, NC), rows], c_ss.at[j], c_rs.at[j], c, t).wait_recv()
        return 0

    lax.fori_loop(1, NROW, c_wait, 0)
    carry1 = [carry[k] for k in range(NC)]
    carry0 = [
        (bs1[:, k * 256:(k + 1) * 256] + jnp.exp(clos[1:2, k * 256:(k + 1) * 256]) * carry1[k].astype(F32)).astype(BF16)
        for k in range(NC)
    ]
    halo = remote(gc.at[pl.ds(0, 8)], gc.at[pl.ds(ROWS, 8)], h_ss, h_rs, prv, t)
    for n in range(NT):
        rows = slice(n * TILE, (n + 1) * TILE)
        for k in range(NC):
            lanes = slice(k * 256, (k + 1) * 256)
            beyond = dot(sin[rows, :], (carry0 if n < NT // 2 else carry1)[k], ((1,), (0,)))
            value = a_ref[rows, lanes] + b_ref[rows, lanes] * beyond
            gc[rows, lanes] = value.astype(BF16).astype(F32)
        if n == 0:
            halo.start()
    for name in ("taps", "vp"):
        loads[name].wait()
    for n in range(NT):
        r0 = n * TILE
        rows = slice(r0, r0 + TILE)
        if n == NT - 1:
            halo.wait_recv()
            gc[ROWS:ROWS + 8, :] = jnp.where(c == NCTX - 1, 0.0, gc[ROWS:ROWS + 8, :])
        summed = taps[0:1, :] * gc[r0 + 3:r0 + 3 + TILE, :]
        for j in range(1, 4):
            summed = summed + taps[j:j + 1, :] * gc[r0 + 3 - j:r0 + 3 - j + TILE, :]
        gp[rows, :] = summed.astype(BF16)
        for k in (1, 3, 2):
            tt = lax.rem(t + k, NX)
            part = dot(gp[rows, :], vp[pl.ds(pl.multiple_of(tt * FEAT, FEAT), FEAT), :], ((1,), (1,)))
            p_send[tt, rows, :] = part.astype(BF16)
            remote(p_send.at[tt, pl.ds(r0, TILE)], x_recv.at[t, pl.ds(r0, TILE)], x_ss.at[n, tt], x_rs.at[n, t], c, tt).start()

    other = 1 - core
    mate = c + 1 - 2 * core

    def w_copy(q):
        return remote(w_send.at[q], w_recv.at[q], w_ss.at[q], w_rs.at[q], mate, t)

    for q in range(Q):
        w_send[q] = dot(lt[other], gp[:, q * QW:(q + 1) * QW], ((1,), (0,))).astype(BF16)
        w_copy(q).start()
    for q in range(Q):
        w_own[q] = dot(lt[core], gp[:, q * QW:(q + 1) * QW], ((1,), (0,)))
    x_own[...] = dot(gp[...], vp[pl.ds(pl.multiple_of(t * FEAT, FEAT), FEAT), :], ((1,), (1,)))

    for q in range(Q):
        w_copy(q).wait_recv()
        for k in (2, 1, 3):
            yy = lax.rem(y + k, NY)
            rows = pl.ds(pl.multiple_of(yy * 128, 128), 128)
            v_send[q, yy] = (w_own[q, rows, :] + w_recv[q, rows, :].astype(F32)).astype(BF16)
            remote(v_send.at[q, yy], v_recv.at[q, y], v_ss.at[q, yy], v_rs.at[q, y], lax.rem(c + k * NROW, NCTX), t).start()
        rows = pl.ds(pl.multiple_of(y * 128, 128), 128)
        u_own[q] = w_own[q, rows, :] + w_recv[q, rows, :].astype(F32)
    for q in range(Q):
        acc = u_own[q]
        for k in range(1, NY):
            yy = lax.rem(y + k, NY)
            remote(v_send.at[q, yy], v_recv.at[q, yy], v_ss.at[q, yy], v_rs.at[q, yy], c, t).wait_recv()
            acc = acc + v_recv[q, yy].astype(F32)
        u_own[q] = acc
        u_send[q] = acc.astype(BF16)

        def u_start(k, _, q=q):
            zz = lax.rem(z + k, NZ)
            rows = pl.ds(pl.multiple_of(zz * 16, 16), 16)
            remote(u_send.at[q, rows], u_recv.at[q, z], u_ss.at[q, zz], u_rs.at[q, z], row0 + zz * NC + core, t).start()
            return 0

        lax.fori_loop(1, NZ, u_start, 0)

    for n in range(NT):
        rows = slice(n * TILE, (n + 1) * TILE)
        acc = x_own[rows, :]
        for k in range(1, NX):
            tt = lax.rem(t + k, NX)
            remote(p_send.at[tt, pl.ds(n * TILE, TILE)], x_recv.at[tt, pl.ds(n * TILE, TILE)], x_ss.at[n, tt], x_rs.at[n, tt], c, tt).wait_recv()
            acc = acc + x_recv[tt, rows, :].astype(F32)
        gi_ref[rows, :] = acc.astype(BF16)

    for q in range(Q):
        def u_add(k, acc, q=q):
            zz = lax.rem(z + k, NZ)
            remote(u_send.at[q, pl.ds(0, 16)], u_recv.at[q, zz], u_ss.at[q, zz], u_rs.at[q, zz], c, t).wait_recv()
            return acc + u_recv[q, zz].astype(F32)

        acc = lax.fori_loop(1, NZ, u_add, u_own[q, my_rows, :])
        gv_ref[:, q * QW:(q + 1) * QW] = acc * (1.0 / math.sqrt(ROWS * NCTX))

    def sent(k, _):
        d_copy(k).wait_send()
        s_copy(k).wait_send()
        c_copy(k).wait_send()
        return 0

    lax.fori_loop(1, NROW, sent, 0)
    for k in range(1, NX):
        tt = lax.rem(t + k, NX)
        remote(lay_h, lay.at[t], lay_ss.at[tt], lay_rs.at[t], c, tt).wait_send()
        for n in range(NT):
            part = pl.ds(n * TILE, TILE)
            remote(p_send.at[tt, part], x_recv.at[t, part], x_ss.at[n, tt], x_rs.at[n, t], c, tt).wait_send()
    halo.wait_send()
    for k in range(1, NY):
        yy = lax.rem(y + k, NY)
        remote(y_send, y_recv.at[y], y_ss.at[yy], y_rs.at[y], c, t).wait_send()
        for q in range(Q):
            remote(v_send.at[q, yy], v_recv.at[q, y], v_ss.at[q, yy], v_rs.at[q, y], c, t).wait_send()
    for q in range(Q):
        w_copy(q).wait_send()

        def u_sent(k, _, q=q):
            zz = lax.rem(z + k, NZ)
            remote(u_send.at[q, pl.ds(0, 16)], u_recv.at[q, z], u_ss.at[q, zz], u_rs.at[q, z], c, t).wait_send()
            return 0

        lax.fori_loop(1, NZ, u_sent, 0)


def local(layer_input, value_proj, conv_taps, conv_pre, state_in, state_out, step_size, log_decay, skip_gain, grad_out):
    dma = pltpu.SemaphoreType.DMA
    V = pltpu.VMEM
    scratch = [
        V((NX, ROWS, FEAT), BF16), V((NX * FEAT, CH), BF16), V((4, CH), F32), V((ROWS, CH), BF16),
        V((ROWS, STATE), BF16), V((ROWS, STATE), BF16), V((HEADS, ROWS), F32), V((HEADS, ROWS), F32),
        V((1, HEADS), F32), V((ROWS, CH), BF16),
        V((HEADS, ROWS), F32), V((ROWS, CH), F32), V((ROWS, CH), F32), V((ROWS + 8, CH), F32), V((ROWS, CH), BF16),
        V((STATE, CH), F32), V((8, CH), F32), V((NC, ROWS, ROWS), BF16),
        V((NC, STATE, 256), BF16), V((NROW, 16, 256), BF16), V((NC, 1, 256), F32), V((NROW, 1, 256), F32),
        V((NROW, 16, 256), F32), V((NROW, 1, 256), F32), V((24, 256), F32), V((NY, 24, 256), F32),
        V((NROW, 16, 256), BF16), V((NC, STATE, 256), BF16),
        V((NX, ROWS, FEAT), BF16), V((NX, ROWS, FEAT), BF16), V((ROWS, FEAT), F32),
        V((Q, 512, QW), BF16), V((Q, 512, QW), BF16), V((Q, 512, QW), F32),
        V((Q, NY, 128, QW), BF16), V((Q, NY, 128, QW), BF16), V((Q, 128, QW), F32),
        V((Q, 128, QW), BF16), V((Q, NZ, 16, QW), BF16),
        dma((10,)), dma((NX,)), dma((NX,)), dma((NROW,)), dma((NROW,)), dma((NROW,)), dma((NROW,)),
        dma((NY,)), dma((NY,)), dma((NROW,)), dma((NROW,)), dma, dma,
        dma((NT, NX)), dma((NT, NX)), dma((Q,)), dma((Q,)), dma((Q, NY)), dma((Q, NY)), dma((Q, NZ)), dma((Q, NZ)),
    ]
    return pl.pallas_call(
        kernel,
        out_shape=(
            jax.ShapeDtypeStruct((ROWS, FEAT), BF16),
            jax.ShapeDtypeStruct((16, CH), F32),
        ),
        in_specs=[pl.BlockSpec(memory_space=pl.ANY)] * 10,
        out_specs=(pl.BlockSpec(memory_space=pltpu.VMEM), pl.BlockSpec(memory_space=pltpu.VMEM)),
        scratch_shapes=scratch,
        compiler_params=pltpu.CompilerParams(
            collective_id=0, has_side_effects=True, vmem_limit_bytes=48 * 2**20
        ),
        cost_estimate=pl.CostEstimate(flops=1_500_000_000, bytes_accessed=4_000_000, transcendentals=2_000_000),
        name="scan_backward",
    )(
        layer_input, value_proj, conv_taps, conv_pre, state_in, state_out, step_size, log_decay,
        skip_gain.reshape(1, HEADS), grad_out,
    )


def solution(mesh):
    return jax.shard_map(
        local,
        mesh=mesh,
        in_specs=(
            P("context", "tensor"),
            P(None, "tensor"),
            P(None, "tensor"),
            P("context", "tensor"),
            P("context", None),
            P("context", None),
            P("tensor", "context"),
            P("tensor", "context"),
            P("tensor"),
            P("context", "tensor"),
        ),
        out_specs=(P("context", "tensor"), P("context", "tensor")),
        check_vma=False,
    )
```

```python
import functools
import math

import jax
import jax.numpy as jnp
from jax import lax
from jax.experimental import pallas as pl
from jax.experimental.pallas import tpu as pltpu
from jax.sharding import PartitionSpec as P

MESH = pl.DeviceIdType.MESH
F32, BF16 = jnp.float32, jnp.bfloat16
HIGH = lax.Precision.HIGHEST

NX, NY, NZ, NC = 4, 4, 8, 2
NROW = NZ * NC
NCTX = NY * NROW
ROWS, CH, STATE, BLOCK, HEADS, HD = 512, 512, 128, 256, 8, 64
FEAT, HALF = 256, 128
Q, QW = 2, 256
TILE, NT = 128, 4
XT, XR = 2, 256


def dot(a, b, dims, precision=None):
    return lax.dot_general(a, b, (dims, ((), ())), precision=precision, preferred_element_type=F32)


def remote(src, dst, send, recv, ctx, ten):
    return pltpu.make_async_remote_copy(
        src_ref=src, dst_ref=dst, send_sem=send, recv_sem=recv,
        device_id=(ctx, ten), device_id_type=MESH,
    )


def kernel(
    lay_h, vp_h, taps_h, pre_h, sin_h, sout_h, step_h, ld_h, skip_h, go_h,
    gi_ref, gv_ref,
    lay, vp, taps, pre, sin, sout, step, ld, skip, go,
    cum, a_ref, b_ref, gc, gp, bs1, clos, lt,
    s_send, s_recv, later, z_send, z_recv, rsuf, lsuf, y_send, y_recv, c_send, c_recv, m_send, carry,
    xo_send, xo_recv, xd_send, xd_recv, x_keep, x_own,
    w_send, w_recv, w_own, vo_send, vo_recv, vd_send, vd_recv, v_keep, u_own, u_send, u_recv,
    in_sem, lay_ss, lay_rs, s_ss, s_rs, z_ss, z_rs, y_ss, y_rs, c_ss, c_rs, m_ss, m_rs, h_ss, h_rs,
    xo_ss, xo_rs, xd_ss, xd_rs, w_ss, w_rs, vo_ss, vo_rs, vd_ss, vd_rs, u_ss, u_rs,
):
    c = lax.axis_index("context")
    t = lax.axis_index("tensor")
    core = lax.rem(c, NC)
    other = 1 - core
    z = lax.rem(c // NC, NZ)
    y = c // NROW
    row0 = y * NROW + core
    nxt, prv = lax.rem(c + 1, NCTX), lax.rem(c + NCTX - 1, NCTX)
    mate = c + 1 - 2 * core
    xs = [lax.rem(t + k, NX) for k in range(NX)]
    ys = [lax.rem(y + k, NY) for k in range(NY)]
    yc = [lax.rem(c + k * NROW, NCTX) for k in range(NY)]
    zs = [lax.rem(z + k, NZ) for k in range(NZ)]
    zc = [row0 + k * NC for k in zs]

    def slab(k, n):
        return pl.ds(pl.multiple_of(k * n, n), n)

    barrier = pltpu.get_barrier_semaphore()
    partners = [(zc[k], t) for k in range(1, NZ)] + [(yc[k], t) for k in range(1, NY)]
    partners += [(c, xs[1]), (c, xs[3]), (nxt, t), (prv, t)]
    for ctx, ten in partners:
        pl.semaphore_signal(barrier, inc=1, device_id=(ctx, ten), device_id_type=MESH)

    loads = {}
    for n, (name, src, dst) in enumerate((
        ("ld", ld_h, ld), ("go", go_h, go), ("sout", sout_h, sout), ("sin", sin_h, sin),
        ("step", step_h, step), ("skip", skip_h, skip), ("pre", pre_h, pre), ("taps", taps_h, taps),
        ("vp", vp_h, vp), ("lay", lay_h, lay.at[t]),
    )):
        loads[name] = pltpu.make_async_copy(src, dst, in_sem.at[n])
        loads[name].start()

    ri = lax.broadcasted_iota(jnp.int32, (BLOCK, BLOCK), 0)
    ci = lax.broadcasted_iota(jnp.int32, (BLOCK, BLOCK), 1)
    upto = (ri <= ci).astype(F32)
    hi = lax.broadcasted_iota(jnp.int32, (HEADS, CH), 0)
    li = lax.broadcasted_iota(jnp.int32, (HEADS, CH), 1)
    onehot = (li // HD == hi).astype(F32)
    loads["ld"].wait()
    for k in range(2):
        cum[:, k * BLOCK:(k + 1) * BLOCK] = dot(ld[:, k * BLOCK:(k + 1) * BLOCK], upto, ((1,), (0,)), HIGH)
    for k in range(2):
        b_ref[k * BLOCK:(k + 1) * BLOCK, :] = dot(cum[:, k * BLOCK:(k + 1) * BLOCK], onehot, ((0,), (0,)), HIGH)
    clos0 = b_ref[BLOCK - 1:BLOCK, :]
    clos1 = b_ref[2 * BLOCK - 1:2 * BLOCK, :]
    clos[0:1, :] = clos0
    clos[1:2, :] = clos1
    for k in range(NC):
        s_send[k, STATE:STATE + 8, :] = jnp.broadcast_to((clos0 + clos1)[:, k * 256:(k + 1) * 256], (8, 256))

    loads["go"].wait()
    loads["sout"].wait()
    state = None
    for k in range(2):
        w = (go[k * BLOCK:(k + 1) * BLOCK, :].astype(F32) * jnp.exp(b_ref[k * BLOCK:(k + 1) * BLOCK, :])).astype(BF16)
        bs = dot(sout[k * BLOCK:(k + 1) * BLOCK, :], w, ((0,), (0,)))
        if k == 0:
            state = bs
        else:
            bs1[...] = bs
            state = state + jnp.exp(clos0) * bs
    for k in range(NC):
        s_send[k, 0:STATE, :] = state[:, k * 256:(k + 1) * 256]

    pl.semaphore_wait(barrier, len(partners))

    s_copy = remote(s_send.at[other], s_recv, s_ss, s_rs, mate, t)
    s_copy.start()

    remote(lay_h, lay.at[t], lay_ss.at[0], lay_rs.at[0], c, xs[1]).start()
    remote(lay_h, lay.at[t], lay_ss.at[1], lay_rs.at[1], c, xs[3]).start()

    def within(k):
        rows = slice(k * BLOCK, (k + 1) * BLOCK)
        scores = dot(sin[rows, :], sout[rows, :], ((1,), (1,)))
        scores = jnp.where(ci >= ri, scores, 0.0)
        low = lax.broadcasted_iota(jnp.int32, (BLOCK, 128), 1) < HD
        cum_t = cum[:, rows].T
        for pair in range(HEADS // 2):
            lanes = slice(pair * 128, pair * 128 + 128)
            g = go[rows, lanes]
            parts = []
            for h in (2 * pair, 2 * pair + 1):
                spread = cum[h:h + 1, rows] - cum_t[:, h:h + 1]
                weights = (scores * jnp.exp(jnp.minimum(spread, 0.0))).astype(BF16)
                parts.append(dot(weights, g, ((1,), (0,))))
            a_ref[rows, lanes] = jnp.where(low, parts[0], parts[1])

    loads["sin"].wait()
    within(0)

    s_copy.wait_recv()
    first = jnp.where(core == 0, s_send[core], s_recv[...])
    second = jnp.where(core == 0, s_recv[...], s_send[core])
    later[...] = second
    d_first, d_second = first[STATE:STATE + 1, :], second[STATE:STATE + 1, :]
    chip = first[0:STATE, :] + jnp.exp(d_first) * second[0:STATE, :]
    z_send[:, 0:256] = chip.astype(BF16)
    d_chip = d_first + d_second
    row = lax.broadcasted_iota(jnp.int32, (16, 128), 0)
    extra = jnp.zeros((16, 128), F32)
    rest = d_chip
    for n in range(3):
        piece = rest.astype(BF16).astype(F32)
        rest = rest - piece
        extra = jnp.where(row == 2 * n, piece[:, 0:128], extra)
        extra = jnp.where(row == 2 * n + 1, piece[:, 128:256], extra)
    extra = extra.astype(BF16)
    for n in range(NZ):
        z_send[n * 16:(n + 1) * 16, 256:384] = extra
    for k in (4, 3, 5, 2, 6, 1, 7):
        remote(z_send.at[slab(zs[k], 16)], z_recv.at[z], z_ss, z_rs, zc[k], t).start()
    z_recv[z] = z_send[slab(z, 16), :]

    within(1)

    remote(z_send.at[pl.ds(0, 112)], z_recv.at[pl.ds(0, NZ - 1)], z_ss, z_rs, c, t).wait_recv()
    r, l = jnp.zeros((16, 256), F32), jnp.zeros((1, 256), F32)
    for j in range(NZ - 1, -1, -1):
        rsuf[j] = r
        lsuf[j] = l
        got = z_recv[j].astype(F32)
        d = jnp.concatenate(
            [got[n:n + 1, 256:384] + got[n + 2:n + 3, 256:384] + got[n + 4:n + 5, 256:384] for n in range(2)], axis=1
        )
        r, l = got[:, 0:256] + jnp.exp(d) * r, l + d
    y_send[0:16, :] = r
    y_send[16:24, :] = jnp.broadcast_to(l, (8, 256))
    for k in (2, 1, 3):
        remote(y_send, y_recv.at[y], y_ss, y_rs, yc[k], t).start()
    y_recv[y] = y_send[...]

    for k, n in ((3, 0), (1, 1)):
        remote(lay_h, lay.at[xs[k]], lay_ss.at[n], lay_rs.at[n], c, t).wait_recv()
        half = pl.ds(n * 256, 256)
        block = lay.at[xs[k], half]
        remote(block, block, lay_ss.at[2 + n], lay_rs.at[2 + n], c, xs[4 - k]).start()

    for name in ("step", "skip", "pre"):
        loads[name].wait()
    skip_e = dot(skip[...], onehot, ((1,), (0,)), HIGH)

    def factors(n):
        rows = slice(n * 64, (n + 1) * 64)
        close = clos[n // 4:n // 4 + 1, :]
        v = pre[rows, :].astype(F32)
        sig = 1.0 / (1.0 + jnp.exp(-v))
        slope = sig * (1.0 + v * (1.0 - sig))
        step_e = dot(step[:, rows], onehot, ((0,), (0,)), HIGH)
        a_ref[rows, :] = (step_e * a_ref[rows, :] + skip_e * go[rows, :].astype(F32)) * slope
        b_ref[rows, :] = step_e * jnp.exp(close - b_ref[rows, :]) * slope

    for n in range(4):
        factors(n)

    remote(y_send, y_recv.at[pl.ds(0, NY - 1)], y_ss, y_rs, c, t).wait_recv()
    coming = jnp.zeros((16, 256), F32)
    for yy in range(NY - 1, 0, -1):
        r = y_recv[yy]
        coming = jnp.where(yy > y, r[0:16, :] + jnp.exp(r[16:17, :]) * coming, coming)
    for j in range(NZ):
        c_send[j * 16:(j + 1) * 16, :] = (rsuf[j] + jnp.exp(lsuf[j]) * coming).astype(BF16)
    for k in (4, 3, 5, 2, 6, 1, 7):
        remote(c_send.at[slab(zs[k], 16)], c_recv.at[slab(z, 16)], c_ss, c_rs, zc[k], t).start()
    c_recv[slab(z, 16), :] = c_send[slab(z, 16), :]

    for n in range(4, 8):
        factors(n)

    def transposed(x):
        for half in range(2):
            cols = slice(half * 256, half * 256 + 256)
            tr = lay[x, cols, :].T
            for zz in range(NZ):
                for cc in range(NC):
                    f0 = (zz * NC + cc) * 16
                    lt[cc, pl.ds(pl.multiple_of(x * 128 + zz * 16, 16), 16), cols] = tr[f0:f0 + 16, :]

    loads["lay"].wait()
    for k in (0, 1, 3):
        transposed(xs[k])

    remote(c_send, c_recv.at[pl.ds(0, 112)], c_ss, c_rs, c, t).wait_recv()
    into_second = c_recv[...]
    into_first = (later[0:STATE, :] + jnp.exp(later[STATE:STATE + 1, :]) * into_second.astype(F32)).astype(BF16)
    m_send[...] = jnp.where(core == 0, into_second, into_first)
    m_copy = remote(m_send, carry.at[core], m_ss, m_rs, mate, t)
    m_copy.start()
    carry[core] = jnp.where(core == 0, into_first, into_second)

    for n, rows in ((0, pl.ds(0, 256)), (1, pl.ds(256, 256))):
        block = lay.at[xs[2], rows]
        remote(block, block, lay_ss.at[2 + n], lay_rs.at[2 + n], c, t).wait_recv()
    transposed(xs[2])
    for name in ("taps", "vp"):
        loads[name].wait()

    remote(m_send, carry.at[other], m_ss, m_rs, mate, t).wait_recv()
    carry1 = [carry[k] for k in range(NC)]
    carry0 = [
        (bs1[:, k * 256:(k + 1) * 256] + jnp.exp(clos[1:2, k * 256:(k + 1) * 256]) * carry1[k].astype(F32)).astype(BF16)
        for k in range(NC)
    ]
    halo = remote(gc.at[pl.ds(0, 8)], gc.at[pl.ds(ROWS, 8)], h_ss, h_rs, prv, t)
    for n in range(NT):
        rows = slice(n * TILE, (n + 1) * TILE)
        for k in range(NC):
            lanes = slice(k * 256, (k + 1) * 256)
            beyond = dot(sin[rows, :], (carry0 if n < NT // 2 else carry1)[k], ((1,), (0,)))
            value = a_ref[rows, lanes] + b_ref[rows, lanes] * beyond
            gc[rows, lanes] = value.astype(BF16).astype(F32)
        if n == 0:
            halo.start()

    def weights_of(k):
        return vp[slab(xs[k], FEAT), :]

    for n in range(XT):
        rows = slice(n * XR, (n + 1) * XR)
        for r0 in range(n * XR, (n + 1) * XR, TILE):
            if r0 == ROWS - TILE:
                halo.wait_recv()
                gc[ROWS:ROWS + 8, :] = jnp.where(c == NCTX - 1, 0.0, gc[ROWS:ROWS + 8, :])
            summed = taps[0:1, :] * gc[r0 + 3:r0 + 3 + TILE, :]
            for j in range(1, 4):
                summed = summed + taps[j:j + 1, :] * gc[r0 + 3 - j:r0 + 3 - j + TILE, :]
            gp[r0:r0 + TILE, :] = summed.astype(BF16)
        part = dot(gp[rows, :], weights_of(2), ((1,), (1,)))
        for s in range(2):
            xo_send[n, s] = part[:, s * HALF:(s + 1) * HALF].astype(BF16)
            remote(xo_send.at[n, s], xo_recv.at[n, s], xo_ss, xo_rs.at[n, s], c, xs[(1, 3)[s]]).start()

    def w_copy(q):
        return remote(w_send.at[q], w_recv.at[q], w_ss.at[q], w_rs.at[q], mate, t)

    for q in range(Q):
        w_send[q] = dot(lt[other], gp[:, q * QW:(q + 1) * QW], ((1,), (0,))).astype(BF16)
        w_copy(q).start()

    def xd_start(n, s, half):
        remote(xd_send.at[n, s, half], xd_recv.at[n, s, half], xd_ss, xd_rs.at[n, s, half], c, xs[(1, 3)[s]]).start()

    for n in range(XT):
        rows = slice(n * XR, (n + 1) * XR)
        for s in range(2):
            part = dot(gp[rows, :], weights_of((1, 3)[s]), ((1,), (1,)))
            xd_send[n, s, 1 - s] = part[:, (1 - s) * HALF:(2 - s) * HALF].astype(BF16)
            xd_start(n, s, 1 - s)
            x_keep[n, s] = part[:, s * HALF:(s + 1) * HALF]

    for q in range(Q):
        w_own[q] = dot(lt[core], gp[:, q * QW:(q + 1) * QW], ((1,), (0,)))

    def vd_start(q, s, half):
        remote(vd_send.at[q, s, half], vd_recv.at[q, s, half], vd_ss, vd_rs.at[q, s, half], yc[(1, 3)[s]], t).start()

    for q in range(Q):
        w_copy(q).wait_recv()

        def both(k, q=q):
            rows = slab(ys[k], 128)
            return w_own[q, rows, :] + w_recv[q, rows, :].astype(F32)

        part = both(2)
        for s in range(2):
            vo_send[q, s] = part[:, s * HALF:(s + 1) * HALF].astype(BF16)
            remote(vo_send.at[q, s], vo_recv.at[q, s], vo_ss, vo_rs.at[q, s], yc[(1, 3)[s]], t).start()
        for s in range(2):
            part = both((1, 3)[s])
            vd_send[q, s, 1 - s] = part[:, (1 - s) * HALF:(2 - s) * HALF].astype(BF16)
            vd_start(q, s, 1 - s)
            v_keep[q, s] = part[:, s * HALF:(s + 1) * HALF]
        u_own[:, q * QW:(q + 1) * QW] = both(0)

    x_own[...] = dot(gp[...], weights_of(0), ((1,), (1,)))

    def x_relay(n):
        for s in range(2):
            remote(xo_send.at[n, s], xo_recv.at[n, s], xo_ss, xo_rs.at[n, s], c, t).wait_recv()
            xd_send[n, s, s] = (x_keep[n, s] + xo_recv[n, s].astype(F32)).astype(BF16)
            xd_start(n, s, s)

    def v_relay(q):
        for s in range(2):
            remote(vo_send.at[q, s], vo_recv.at[q, s], vo_ss, vo_rs.at[q, s], c, t).wait_recv()
            vd_send[q, s, s] = (v_keep[q, s] + vo_recv[q, s].astype(F32)).astype(BF16)
            vd_start(q, s, s)

    x_relay(0)
    v_relay(0)
    x_relay(1)
    v_relay(1)

    for q in range(Q):
        for half in range(2):
            lanes = slice(q * QW + half * HALF, q * QW + (half + 1) * HALF)
            acc = u_own[:, lanes]
            for s in range(2):
                remote(vd_send.at[q, s, half], vd_recv.at[q, s, half], vd_ss, vd_rs.at[q, s, half], c, t).wait_recv()
                acc = acc + vd_recv[q, s, half].astype(F32)
            u_own[:, lanes] = acc
            u_send[:, lanes] = acc.astype(BF16)
    for k in (4, 3, 5, 2, 6, 1, 7):
        remote(u_send.at[slab(zs[k], 16)], u_recv.at[z], u_ss, u_rs, zc[k], t).start()
    u_recv[z] = jnp.zeros((16, CH), BF16)

    for n in range(XT):
        rows = slice(n * XR, (n + 1) * XR)
        for half in range(2):
            lanes = slice(half * HALF, (half + 1) * HALF)
            acc = x_own[rows, lanes]
            for s in range(2):
                remote(xd_send.at[n, s, half], xd_recv.at[n, s, half], xd_ss, xd_rs.at[n, s, half], c, t).wait_recv()
                acc = acc + xd_recv[n, s, half].astype(F32)
            gi_ref[rows, lanes] = acc.astype(BF16)

    remote(u_send.at[pl.ds(0, 112)], u_recv.at[pl.ds(0, NZ - 1)], u_ss, u_rs, c, t).wait_recv()
    acc = u_own[slab(z, 16), :]
    for k in range(NZ):
        acc = acc + u_recv[k].astype(F32)
    gv_ref[...] = acc * (1.0 / math.sqrt(ROWS * NCTX))

    def sent(src, sem):
        remote(src, src, sem, h_rs, c, t).wait_send()

    sent(s_send.at[other], s_ss)
    sent(lay_h, lay_ss.at[0])
    sent(lay_h, lay_ss.at[1])
    sent(lay.at[0, pl.ds(0, 256)], lay_ss.at[2])
    sent(lay.at[0, pl.ds(0, 256)], lay_ss.at[3])
    sent(z_send.at[pl.ds(0, 112)], z_ss)
    sent(y_recv.at[pl.ds(0, NY - 1)], y_ss)
    sent(c_send.at[pl.ds(0, 112)], c_ss)
    sent(m_send, m_ss)
    sent(gc.at[pl.ds(0, 8)], h_ss)
    sent(xo_send, xo_ss)
    sent(xd_send, xd_ss)
    for q in range(Q):
        w_copy(q).wait_send()
    sent(vo_send, vo_ss)
    sent(vd_send, vd_ss)
    sent(u_send.at[pl.ds(0, 112)], u_ss)


def place(gi, gv, gi_out, gv_out, sem):
    copies = [pltpu.make_async_copy(gi, gi_out, sem.at[0]), pltpu.make_async_copy(gv, gv_out, sem.at[1])]
    for copy in copies:
        copy.start()
    for copy in copies:
        copy.wait()


def local(layer_input, value_proj, conv_taps, conv_pre, state_in, state_out, step_size, log_decay, skip_gain, grad_out):
    dma = pltpu.SemaphoreType.DMA
    V = pltpu.VMEM
    scratch = [
        V((NX, ROWS, FEAT), BF16), V((NX * FEAT, CH), BF16), V((4, CH), F32), V((ROWS, CH), BF16),
        V((ROWS, STATE), BF16), V((ROWS, STATE), BF16), V((HEADS, ROWS), F32), V((HEADS, ROWS), F32),
        V((1, HEADS), F32), V((ROWS, CH), BF16),
        V((HEADS, ROWS), F32), V((ROWS, CH), F32), V((ROWS, CH), F32), V((ROWS + 8, CH), F32), V((ROWS, CH), BF16),
        V((STATE, CH), F32), V((8, CH), F32), V((NC, ROWS, ROWS), BF16),
        V((NC, STATE + 8, 256), F32), V((STATE + 8, 256), F32), V((STATE + 8, 256), F32),
        V((STATE, 384), BF16), V((NZ, 16, 384), BF16), V((NZ, 16, 256), F32), V((NZ, 1, 256), F32),
        V((24, 256), F32), V((NY, 24, 256), F32),
        V((STATE, 256), BF16), V((STATE, 256), BF16), V((STATE, 256), BF16), V((NC, STATE, 256), BF16),
        V((XT, 2, XR, HALF), BF16), V((XT, 2, XR, HALF), BF16), V((XT, 2, 2, XR, HALF), BF16), V((XT, 2, 2, XR, HALF), BF16),
        V((XT, 2, XR, HALF), F32), V((ROWS, FEAT), F32),
        V((Q, 512, QW), BF16), V((Q, 512, QW), BF16), V((Q, 512, QW), F32),
        V((Q, 2, 128, HALF), BF16), V((Q, 2, 128, HALF), BF16), V((Q, 2, 2, 128, HALF), BF16), V((Q, 2, 2, 128, HALF), BF16),
        V((Q, 2, 128, HALF), F32), V((128, CH), F32), V((128, CH), BF16), V((NZ, 16, CH), BF16),
        dma((10,)), dma((4,)), dma((4,)), dma, dma, dma, dma, dma, dma, dma, dma, dma, dma, dma, dma,
        dma, dma((XT, 2)), dma, dma((XT, 2, 2)), dma((Q,)), dma((Q,)), dma, dma((Q, 2)), dma, dma((Q, 2, 2)), dma, dma,
    ]
    outs = (jax.ShapeDtypeStruct((ROWS, FEAT), BF16), jax.ShapeDtypeStruct((16, CH), F32))
    gi, gv = pl.pallas_call(
        kernel,
        out_shape=outs,
        in_specs=[pl.BlockSpec(memory_space=pl.ANY)] * 10,
        out_specs=(pl.BlockSpec(memory_space=pltpu.VMEM), pl.BlockSpec(memory_space=pltpu.VMEM)),
        scratch_shapes=scratch,
        compiler_params=pltpu.CompilerParams(
            collective_id=0, has_side_effects=True, vmem_limit_bytes=60 * 2**20
        ),
        cost_estimate=pl.CostEstimate(flops=1_500_000_000, bytes_accessed=4_000_000, transcendentals=2_000_000),
        name="scan_backward",
    )(
        layer_input, value_proj, conv_taps, conv_pre, state_in, state_out, step_size, log_decay,
        skip_gain.reshape(1, HEADS), grad_out,
    )
    return pl.pallas_call(
        place,
        out_shape=outs,
        in_specs=[pl.BlockSpec(memory_space=pl.ANY)] * 2,
        out_specs=(pl.BlockSpec(memory_space=pl.ANY), pl.BlockSpec(memory_space=pl.ANY)),
        scratch_shapes=[dma((2,))],
        name="place_outputs",
    )(gi, gv)


def solution(mesh):
    return jax.shard_map(
        local,
        mesh=mesh,
        in_specs=(
            P("context", "tensor"),
            P(None, "tensor"),
            P(None, "tensor"),
            P("context", "tensor"),
            P("context", None),
            P("context", None),
            P("tensor", "context"),
            P("tensor", "context"),
            P("tensor"),
            P("context", "tensor"),
        ),
        out_specs=(P("context", "tensor"), P("context", "tensor")),
        check_vma=False,
    )
```

```python
import functools
import math

import jax
import jax.numpy as jnp
from jax import lax
from jax.experimental import pallas as pl
from jax.experimental.pallas import tpu as pltpu
from jax.sharding import PartitionSpec as P

MESH = pl.DeviceIdType.MESH
F32, BF16 = jnp.float32, jnp.bfloat16
HIGH = lax.Precision.HIGHEST

NX, NY, NZ, NC = 4, 4, 8, 2
NROW = NZ * NC
NCTX = NY * NROW
ROWS, CH, STATE, BLOCK, HEADS, HD = 512, 512, 128, 256, 8, 64
FEAT, HALF = 256, 128
Q, QW = 4, 128
ZFIRST = 3
TILE, NT = 128, 4
XT, XR = 2, 256


def dot(a, b, dims, precision=None):
    return lax.dot_general(a, b, (dims, ((), ())), precision=precision, preferred_element_type=F32)


def remote(src, dst, send, recv, ctx, ten):
    return pltpu.make_async_remote_copy(
        src_ref=src, dst_ref=dst, send_sem=send, recv_sem=recv,
        device_id=(ctx, ten), device_id_type=MESH,
    )


def kernel(
    lay_h, vp_h, taps_h, pre_h, sin_h, sout_h, step_h, ld_h, skip_h, go_h,
    gi_ref, gv_ref,
    lay, vp, taps, pre, sin, sout, step, ld, skip, go,
    cum, a_ref, b_ref, gc, gp, bs1, clos, lt,
    s_send, s_recv, later, z_send, z_recv, rsuf, lsuf, y_send, y_recv, c_send, c_recv, m_send, carry,
    xo_send, xo_recv, xd_send, xd_recv, x_keep, x_own,
    w_acc, w_send, w_recv, w_own, v_send, v_recv, u_own, u_send, u_recv, zf_send, zf_recv, zf_own, yf_send, yf_recv,
    in_sem, lay_ss, lay_rs, s_ss, s_rs, z_ss, z_rs, y_ss, y_rs, c_ss, c_rs, m_ss, m_rs, h_ss, h_rs,
    xo_ss, xo_rs, xd_ss, xd_rs, w_ss, w_rs, v_ss, v_rs, u_ss, u_rs, zf_ss, zf_rs, yf_ss, yf_rs,
):
    c = lax.axis_index("context")
    t = lax.axis_index("tensor")
    core = lax.rem(c, NC)
    other = 1 - core
    z = lax.rem(c // NC, NZ)
    y = c // NROW
    row0 = y * NROW + core
    nxt, prv = lax.rem(c + 1, NCTX), lax.rem(c + NCTX - 1, NCTX)
    mate = c + 1 - 2 * core
    xs = [lax.rem(t + k, NX) for k in range(NX)]
    ys = [lax.rem(y + k, NY) for k in range(NY)]
    yc = [lax.rem(c + k * NROW, NCTX) for k in range(NY)]
    zs = [lax.rem(z + k, NZ) for k in range(NZ)]
    zc = [row0 + k * NC for k in zs]

    def slab(k, n):
        return pl.ds(pl.multiple_of(k * n, n), n)

    loads = {}

    def load(name, src, dst):
        loads[name] = pltpu.make_async_copy(src, dst, in_sem.at[len(loads)])
        loads[name].start()

    load("ld", ld_h, ld)
    load("go", go_h, go)
    load("sout", sout_h, sout)

    barrier = pltpu.get_barrier_semaphore()
    partners = [(zc[k], t) for k in range(1, NZ)] + [(yc[k], t) for k in range(1, NY)]
    partners += [(c, xs[1]), (c, xs[3]), (nxt, t), (prv, t)]
    for ctx, ten in partners:
        pl.semaphore_signal(barrier, inc=1, device_id=(ctx, ten), device_id_type=MESH)

    load("sin", sin_h, sin)
    load("step", step_h, step)
    load("skip", skip_h, skip)
    load("pre", pre_h, pre)
    load("taps", taps_h, taps)
    load("vp", vp_h, vp)
    load("lay", lay_h, lay.at[t])

    def pieces(v):
        parts = []
        for _ in range(3):
            parts.append(v.astype(BF16))
            v = v - parts[-1].astype(F32)
        return parts

    ri = lax.broadcasted_iota(jnp.int32, (BLOCK, BLOCK), 0)
    ci = lax.broadcasted_iota(jnp.int32, (BLOCK, BLOCK), 1)
    upto = jnp.where(ri <= ci, 1.0, 0.0).astype(BF16)
    hi = lax.broadcasted_iota(jnp.int32, (HEADS, CH), 0)
    li = lax.broadcasted_iota(jnp.int32, (HEADS, CH), 1)
    onehot = (li // HD == hi).astype(F32)
    hi3 = lax.broadcasted_iota(jnp.int32, (3 * HEADS, CH), 0)
    li3 = lax.broadcasted_iota(jnp.int32, (3 * HEADS, CH), 1)
    onehot3 = jnp.where(li3 // HD == lax.rem(hi3, HEADS), 1.0, 0.0).astype(BF16)
    loads["ld"].wait()
    for k in range(2):
        cols = slice(k * BLOCK, (k + 1) * BLOCK)
        sums = [dot(p, upto, ((1,), (0,))) for p in pieces(ld[:, cols])]
        cum[:, cols] = (sums[2] + sums[1]) + sums[0]
    cum3 = jnp.concatenate([p.astype(F32) for p in pieces(cum[...])], axis=0).astype(BF16)
    for k in range(2):
        rows = slice(k * BLOCK, (k + 1) * BLOCK)
        b_ref[rows, :] = dot(cum3[:, rows], onehot3, ((0,), (0,)))
    clos0 = b_ref[BLOCK - 1:BLOCK, :]
    clos1 = b_ref[2 * BLOCK - 1:2 * BLOCK, :]
    clos[0:1, :] = clos0
    clos[1:2, :] = clos1
    for k in range(NC):
        s_send[k, STATE:STATE + 8, :] = jnp.broadcast_to((clos0 + clos1)[:, k * 256:(k + 1) * 256], (8, 256))

    loads["go"].wait()
    loads["sout"].wait()
    s_copy = remote(s_send.at[other], s_recv, s_ss, s_rs, mate, t)
    for half in (other, core):
        lanes = slab(half, 256)
        states = []
        for k in range(2):
            rows = slice(k * BLOCK, (k + 1) * BLOCK)
            w = (go[rows, lanes].astype(F32) * jnp.exp(b_ref[rows, lanes])).astype(BF16)
            states.append(dot(sout[rows, :], w, ((0,), (0,))))
        bs1[:, lanes] = states[1]
        s_send[half, 0:STATE, :] = states[0] + jnp.exp(clos[0:1, lanes]) * states[1]
        if half is other:
            pl.semaphore_wait(barrier, len(partners))
            s_copy.start()

    remote(lay_h, lay.at[t], lay_ss.at[0], lay_rs.at[0], c, xs[1]).start()
    remote(lay_h, lay.at[t], lay_ss.at[1], lay_rs.at[1], c, xs[3]).start()

    def within(k):
        rows = slice(k * BLOCK, (k + 1) * BLOCK)
        scores = dot(sin[rows, :], sout[rows, :], ((1,), (1,)))
        scores = jnp.where(ci >= ri, scores, 0.0)
        low = lax.broadcasted_iota(jnp.int32, (BLOCK, 128), 1) < HD
        cum_t = cum[:, rows].T
        for pair in range(HEADS // 2):
            lanes = slice(pair * 128, pair * 128 + 128)
            g = go[rows, lanes]
            parts = []
            for h in (2 * pair, 2 * pair + 1):
                spread = cum[h:h + 1, rows] - cum_t[:, h:h + 1]
                weights = (scores * jnp.exp(jnp.minimum(spread, 0.0))).astype(BF16)
                parts.append(dot(weights, g, ((1,), (0,))))
            a_ref[rows, lanes] = jnp.where(low, parts[0], parts[1])

    loads["sin"].wait()
    within(0)

    s_copy.wait_recv()
    first = jnp.where(core == 0, s_send[core], s_recv[...])
    second = jnp.where(core == 0, s_recv[...], s_send[core])
    later[...] = second
    d_first, d_second = first[STATE:STATE + 1, :], second[STATE:STATE + 1, :]
    chip = first[0:STATE, :] + jnp.exp(d_first) * second[0:STATE, :]
    z_send[:, 0:256] = chip.astype(BF16)
    d_chip = d_first + d_second
    row = lax.broadcasted_iota(jnp.int32, (16, 128), 0)

    def packed(d):
        out = jnp.zeros((16, 128), F32)
        for n, piece in enumerate(pieces(d)):
            piece = piece.astype(F32)
            out = jnp.where(row == 2 * n, piece[:, 0:128], out)
            out = jnp.where(row == 2 * n + 1, piece[:, 128:256], out)
        return out.astype(BF16)

    def unpacked(got):
        return jnp.concatenate([got[n:n + 1, :] + got[n + 2:n + 3, :] + got[n + 4:n + 5, :] for n in range(2)], axis=1)

    extra = packed(d_chip)
    for n in range(NZ):
        z_send[n * 16:(n + 1) * 16, 256:384] = extra
    for k in (4, 3, 5, 2, 6, 1, 7):
        remote(z_send.at[slab(zs[k], 16)], z_recv.at[z], z_ss, z_rs, zc[k], t).start()
    z_recv[z] = z_send[slab(z, 16), :]

    within(1)

    remote(z_send.at[pl.ds(0, 112)], z_recv.at[pl.ds(0, NZ - 1)], z_ss, z_rs, c, t).wait_recv()
    spans = [unpacked(z_recv[j][:, 256:384].astype(F32)) for j in range(NZ)]
    decays = [jnp.exp(d) for d in spans]
    r = jnp.zeros((16, 256), F32)
    for j in range(NZ - 1, -1, -1):
        rsuf[j] = r
        r = z_recv[j][:, 0:256].astype(F32) + decays[j] * r
    y_send[:, 0:256] = r.astype(BF16)
    y_send[:, 256:384] = packed(sum(spans[1:], spans[0]))
    for k in (2, 1, 3):
        remote(y_send, y_recv.at[y], y_ss, y_rs, yc[k], t).start()
    y_recv[y] = y_send[...]
    l = jnp.zeros((1, 256), F32)
    for j in range(NZ - 1, -1, -1):
        lsuf[j] = jnp.exp(l)
        l = l + spans[j]

    for k, n in ((3, 0), (1, 1)):
        remote(lay_h, lay.at[xs[k]], lay_ss.at[n], lay_rs.at[n], c, t).wait_recv()
        half = pl.ds(n * 256, 256)
        block = lay.at[xs[k], half]
        remote(block, block, lay_ss.at[2 + n], lay_rs.at[2 + n], c, xs[4 - k]).start()

    for name in ("step", "skip", "pre"):
        loads[name].wait()
    skip_e = dot(skip[...], onehot, ((1,), (0,)), HIGH)

    def factors(n):
        rows = slice(n * 64, (n + 1) * 64)
        close = clos[n // 4:n // 4 + 1, :]
        v = pre[rows, :].astype(F32)
        sig = 1.0 / (1.0 + jnp.exp(-v))
        slope = sig * (1.0 + v * (1.0 - sig))
        step_e = dot(step[:, rows], onehot, ((0,), (0,)), HIGH)
        a_ref[rows, :] = (step_e * a_ref[rows, :] + skip_e * go[rows, :].astype(F32)) * slope
        b_ref[rows, :] = step_e * jnp.exp(close - b_ref[rows, :]) * slope

    for n in range(4):
        factors(n)

    remote(y_send, y_recv.at[pl.ds(0, NY - 1)], y_ss, y_rs, c, t).wait_recv()
    coming = jnp.zeros((16, 256), F32)
    for yy in range(NY - 1, 0, -1):
        got = y_recv[yy].astype(F32)
        coming = jnp.where(yy > y, got[:, 0:256] + jnp.exp(unpacked(got[:, 256:384])) * coming, coming)
    for k in (4, 3, 5, 2, 6, 1, 7, 0):
        c_send[slab(zs[k], 16), :] = (rsuf[zs[k]] + lsuf[zs[k]] * coming).astype(BF16)
        if k:
            remote(c_send.at[slab(zs[k], 16)], c_recv.at[slab(z, 16)], c_ss, c_rs, zc[k], t).start()
    c_recv[slab(z, 16), :] = c_send[slab(z, 16), :]

    for n in range(4, 8):
        factors(n)

    def transposed(x):
        for half in range(2):
            cols = slice(half * 256, half * 256 + 256)
            tr = lay[x, cols, :].T
            for zz in range(NZ):
                for cc in range(NC):
                    f0 = (zz * NC + cc) * 16
                    lt[cc, pl.ds(pl.multiple_of(x * 128 + zz * 16, 16), 16), cols] = tr[f0:f0 + 16, :]

    loads["lay"].wait()
    for k in (0, 1, 3):
        transposed(xs[k])
    for n, rows in ((0, pl.ds(0, 256)), (1, pl.ds(256, 256))):
        block = lay.at[xs[2], rows]
        remote(block, block, lay_ss.at[2 + n], lay_rs.at[2 + n], c, t).wait_recv()
    transposed(xs[2])
    for name in ("taps", "vp"):
        loads[name].wait()
    decay_second = jnp.exp(later[STATE:STATE + 1, :])

    remote(c_send, c_recv.at[pl.ds(0, 112)], c_ss, c_rs, c, t).wait_recv()
    into_second = c_recv[...]
    into_first = (later[0:STATE, :] + decay_second * into_second.astype(F32)).astype(BF16)
    m_send[...] = jnp.where(core == 0, into_second, into_first)
    m_copy = remote(m_send, carry.at[core], m_ss, m_rs, mate, t)
    m_copy.start()
    carry[core] = jnp.where(core == 0, into_first, into_second)

    halo = remote(gc.at[pl.ds(0, 8)], gc.at[pl.ds(ROWS, 8)], h_ss, h_rs, prv, t)

    def conv_grad(rows, lanes, carried):
        value = a_ref[rows, lanes] + b_ref[rows, lanes] * dot(sin[rows, :], carried, ((1,), (0,)))
        gc[rows, lanes] = value.astype(BF16).astype(F32)

    for half in (core, other):
        lanes = slab(half, 256)
        if half is other:
            remote(m_send, carry.at[other], m_ss, m_rs, mate, t).wait_recv()
        into_last = carry[half]
        into_block = (bs1[:, lanes] + jnp.exp(clos[1:2, lanes]) * into_last.astype(F32)).astype(BF16)
        conv_grad(slice(0, 16), lanes, into_block)
        if half is other:
            halo.start()
        conv_grad(slice(16, TILE), lanes, into_block)
        for n in range(1, NT):
            conv_grad(slice(n * TILE, (n + 1) * TILE), lanes, into_block if n < NT // 2 else into_last)

    def weights_of(k):
        return vp[slab(xs[k], FEAT), :]

    def proj_grad(n):
        r0 = n * TILE
        summed = taps[0:1, :] * gc[r0 + 3:r0 + 3 + TILE, :]
        for j in range(1, 4):
            summed = summed + taps[j:j + 1, :] * gc[r0 + 3 - j:r0 + 3 - j + TILE, :]
        gp[r0:r0 + TILE, :] = summed.astype(BF16)

    def far_start(n):
        part = dot(gp[n * XR:(n + 1) * XR, :], weights_of(2), ((1,), (1,)))
        for s in range(2):
            xo_send[n, s] = part[:, s * HALF:(s + 1) * HALF].astype(BF16)
            remote(xo_send.at[n, s], xo_recv.at[n, s], xo_ss, xo_rs.at[n, s], c, xs[(1, 3)[s]]).start()

    proj_grad(0)
    proj_grad(1)
    far_start(0)
    proj_grad(2)
    early = (NT - 1) * TILE
    for h in range(2):
        lanes = slice(h * 256, (h + 1) * 256)
        w_acc[:, lanes] = dot(lt[other, :, 0:early], gp[0:early, lanes], ((1,), (0,)))
    halo.wait_recv()
    gc[ROWS:ROWS + 8, :] = jnp.where(c == NCTX - 1, 0.0, gc[ROWS:ROWS + 8, :])
    proj_grad(3)

    def w_copy(q):
        return remote(w_send.at[q], w_recv.at[q], w_ss.at[q], w_rs.at[q], mate, t)

    for h in range(2):
        lanes = slice(h * 256, (h + 1) * 256)
        part = w_acc[:, lanes] + dot(lt[other, :, early:ROWS], gp[early:ROWS, lanes], ((1,), (0,)))
        for q in (2 * h, 2 * h + 1):
            w_send[q] = part[:, (q % 2) * QW:(q % 2 + 1) * QW].astype(BF16)
            w_copy(q).start()
    far_start(1)

    def xd_start(n, s, half):
        remote(xd_send.at[n, s, half], xd_recv.at[n, s, half], xd_ss, xd_rs.at[n, s, half], c, xs[(1, 3)[s]]).start()

    def near_start(n):
        for s in range(2):
            part = dot(gp[n * XR:(n + 1) * XR, :], weights_of((1, 3)[s]), ((1,), (1,)))
            xd_send[n, s, 1 - s] = part[:, (1 - s) * HALF:(2 - s) * HALF].astype(BF16)
            xd_start(n, s, 1 - s)
            x_keep[n, s] = part[:, s * HALF:(s + 1) * HALF]

    near_start(0)
    for h in range(2):
        part = dot(lt[core], gp[:, h * 256:(h + 1) * 256], ((1,), (0,)))
        for q in (2 * h, 2 * h + 1):
            w_own[q] = part[:, (q % 2) * QW:(q % 2 + 1) * QW]

    for q in (0, ZFIRST, 1, 2):
        w_copy(q).wait_recv()
        w_own[q] = w_own[q] + w_recv[q].astype(F32)
        if q == ZFIRST:
            for zz in range(NZ):
                for yy in range(NY):
                    r0 = yy * 128 + zz * 16
                    zf_send[zz, yy * 16:(yy + 1) * 16, :] = w_own[q, r0:r0 + 16, :].astype(BF16)
            for k in (4, 3, 5, 2, 6, 1, 7):
                remote(zf_send.at[zs[k]], zf_recv.at[z], zf_ss, zf_rs, zc[k], t).start()
        else:
            for k in (2, 1, 3):
                v_send[q, ys[k]] = w_own[q, slab(ys[k], 128), :].astype(BF16)
                remote(v_send.at[q, ys[k]], v_recv.at[q, y], v_ss.at[q], v_rs.at[q], yc[k], t).start()
    near_start(1)
    x_own[...] = dot(gp[...], weights_of(0), ((1,), (1,)))

    for n in range(XT):
        for s in range(2):
            remote(xo_send.at[n, s], xo_recv.at[n, s], xo_ss, xo_rs.at[n, s], c, t).wait_recv()
            xd_send[n, s, s] = (x_keep[n, s] + xo_recv[n, s].astype(F32)).astype(BF16)
            xd_start(n, s, s)

    def to_z(q):
        remote(v_send.at[q, pl.ds(0, NY - 1)], v_recv.at[q, pl.ds(0, NY - 1)], v_ss.at[q], v_rs.at[q], c, t).wait_recv()
        acc = w_own[q, slab(y, 128), :]
        for k in range(1, NY):
            acc = acc + v_recv[q, ys[k]].astype(F32)
        u_own[q] = acc
        u_send[q] = acc.astype(BF16)
        for k in (4, 3, 5, 2, 6, 1, 7):
            remote(u_send.at[q, slab(zs[k], 16)], u_recv.at[q, z], u_ss.at[q], u_rs.at[q], zc[k], t).start()

    def to_y():
        remote(zf_send.at[pl.ds(0, NZ - 1)], zf_recv.at[pl.ds(0, NZ - 1)], zf_ss, zf_rs, c, t).wait_recv()
        acc = jnp.concatenate([w_own[ZFIRST, pl.ds(pl.multiple_of(yy * 128 + z * 16, 16), 16), :] for yy in range(NY)], axis=0)
        for k in range(1, NZ):
            acc = acc + zf_recv[zs[k]].astype(F32)
        zf_own[...] = acc
        yf_send[...] = acc.astype(BF16)
        for k in (2, 1, 3):
            remote(yf_send.at[slab(ys[k], 16)], yf_recv.at[y], yf_ss, yf_rs, yc[k], t).start()

    to_z(0)
    to_z(1)
    to_y()
    to_z(2)

    for n in range(XT):
        rows = slice(n * XR, (n + 1) * XR)
        for half in range(2):
            lanes = slice(half * HALF, (half + 1) * HALF)
            acc = x_own[rows, lanes]
            for s in range(2):
                remote(xd_send.at[n, s, half], xd_recv.at[n, s, half], xd_ss, xd_rs.at[n, s, half], c, t).wait_recv()
                acc = acc + xd_recv[n, s, half].astype(F32)
            gi_ref[rows, lanes] = acc.astype(BF16)

    scale = 1.0 / math.sqrt(ROWS * NCTX)
    for q in (0, 1, ZFIRST, 2):
        if q == ZFIRST:
            remote(yf_send.at[pl.ds(0, 48)], yf_recv.at[pl.ds(0, NY - 1)], yf_ss, yf_rs, c, t).wait_recv()
            acc = zf_own[slab(y, 16), :]
            for k in range(1, NY):
                acc = acc + yf_recv[ys[k]].astype(F32)
        else:
            remote(u_send.at[q, pl.ds(0, 112)], u_recv.at[q, pl.ds(0, NZ - 1)], u_ss.at[q], u_rs.at[q], c, t).wait_recv()
            acc = u_own[q, slab(z, 16), :]
            for k in range(1, NZ):
                acc = acc + u_recv[q, zs[k]].astype(F32)
        gv_ref[:, q * QW:(q + 1) * QW] = acc * scale

    def sent(src, sem):
        remote(src, src, sem, h_rs, c, t).wait_send()

    sent(s_send.at[other], s_ss)
    sent(lay_h, lay_ss.at[0])
    sent(lay_h, lay_ss.at[1])
    sent(lay.at[0, pl.ds(0, 256)], lay_ss.at[2])
    sent(lay.at[0, pl.ds(0, 256)], lay_ss.at[3])
    sent(z_send.at[pl.ds(0, 112)], z_ss)
    sent(y_recv.at[pl.ds(0, NY - 1)], y_ss)
    sent(c_send.at[pl.ds(0, 112)], c_ss)
    sent(m_send, m_ss)
    sent(gc.at[pl.ds(0, 8)], h_ss)
    sent(xo_send, xo_ss)
    sent(xd_send, xd_ss)
    for q in range(Q):
        w_copy(q).wait_send()
        if q != ZFIRST:
            sent(v_send.at[q, pl.ds(0, NY - 1)], v_ss.at[q])
            sent(u_send.at[q, pl.ds(0, 112)], u_ss.at[q])
    sent(zf_send.at[pl.ds(0, NZ - 1)], zf_ss)
    sent(yf_send.at[pl.ds(0, 48)], yf_ss)


def local(layer_input, value_proj, conv_taps, conv_pre, state_in, state_out, step_size, log_decay, skip_gain, grad_out):
    dma = pltpu.SemaphoreType.DMA
    V = pltpu.VMEM
    scratch = [
        V((NX, ROWS, FEAT), BF16), V((NX * FEAT, CH), BF16), V((4, CH), F32), V((ROWS, CH), BF16),
        V((ROWS, STATE), BF16), V((ROWS, STATE), BF16), V((HEADS, ROWS), F32), V((HEADS, ROWS), F32),
        V((1, HEADS), F32), V((ROWS, CH), BF16),
        V((HEADS, ROWS), F32), V((ROWS, CH), F32), V((ROWS, CH), F32), V((ROWS + 8, CH), F32), V((ROWS, CH), BF16),
        V((STATE, CH), F32), V((8, CH), F32), V((NC, ROWS, ROWS), BF16),
        V((NC, STATE + 8, 256), F32), V((STATE + 8, 256), F32), V((STATE + 8, 256), F32),
        V((STATE, 384), BF16), V((NZ, 16, 384), BF16), V((NZ, 16, 256), F32), V((NZ, 1, 256), F32),
        V((16, 384), BF16), V((NY, 16, 384), BF16),
        V((STATE, 256), BF16), V((STATE, 256), BF16), V((STATE, 256), BF16), V((NC, STATE, 256), BF16),
        V((XT, 2, XR, HALF), BF16), V((XT, 2, XR, HALF), BF16), V((XT, 2, 2, XR, HALF), BF16), V((XT, 2, 2, XR, HALF), BF16),
        V((XT, 2, XR, HALF), F32), V((ROWS, FEAT), F32),
        V((512, CH), F32), V((Q, 512, QW), BF16), V((Q, 512, QW), BF16), V((Q, 512, QW), F32),
        V((Q, NY, 128, QW), BF16), V((Q, NY, 128, QW), BF16), V((Q, 128, QW), F32), V((Q, 128, QW), BF16), V((Q, NZ, 16, QW), BF16),
        V((NZ, 64, QW), BF16), V((NZ, 64, QW), BF16), V((64, QW), F32), V((64, QW), BF16), V((NY, 16, QW), BF16),
        dma((10,)), dma((4,)), dma((4,)), dma, dma, dma, dma, dma, dma, dma, dma, dma, dma, dma, dma,
        dma, dma((XT, 2)), dma, dma((XT, 2, 2)), dma((Q,)), dma((Q,)), dma((Q,)), dma((Q,)), dma((Q,)), dma((Q,)), dma, dma, dma, dma,
    ]
    outs = (V((ROWS, FEAT), BF16), V((16, CH), F32))
    return pl.pallas_call(
        kernel,
        out_shape=outs,
        in_specs=[pl.BlockSpec(memory_space=pl.ANY)] * 10,
        out_specs=(pl.BlockSpec(memory_space=pltpu.VMEM), pl.BlockSpec(memory_space=pltpu.VMEM)),
        scratch_shapes=scratch,
        compiler_params=pltpu.CompilerParams(
            collective_id=0, has_side_effects=True, vmem_limit_bytes=60 * 2**20
        ),
        cost_estimate=pl.CostEstimate(flops=1_500_000_000, bytes_accessed=4_000_000, transcendentals=2_000_000),
        name="scan_backward",
    )(
        layer_input, value_proj, conv_taps, conv_pre, state_in, state_out, step_size, log_decay,
        skip_gain.reshape(1, HEADS), grad_out,
    )


def solution(mesh):
    return jax.shard_map(
        local,
        mesh=mesh,
        in_specs=(
            P("context", "tensor"),
            P(None, "tensor"),
            P(None, "tensor"),
            P("context", "tensor"),
            P("context", None),
            P("context", None),
            P("tensor", "context"),
            P("tensor", "context"),
            P("tensor"),
            P("context", "tensor"),
        ),
        out_specs=(P("context", "tensor"), P("context", "tensor")),
        check_vma=False,
    )
```

```python
import functools
import math

import jax
import jax.numpy as jnp
from jax import lax
from jax.experimental import pallas as pl
from jax.experimental.pallas import tpu as pltpu
from jax.sharding import PartitionSpec as P

MESH = pl.DeviceIdType.MESH
F32, BF16 = jnp.float32, jnp.bfloat16
HIGH = lax.Precision.HIGHEST

NX, NY, NZ, NC = 4, 4, 8, 2
NROW = NZ * NC
NCTX = NY * NROW
ROWS, CH, STATE, BLOCK, HEADS, HD = 512, 512, 128, 256, 8, 64
FEAT, HALF = 256, 128
Q, QW = 4, 128
ZFIRST = 3
TILE, NT = 128, 4
PIECES = ((0, 256), (256, 240), (496, 16))


def dot(a, b, dims, precision=None):
    return lax.dot_general(a, b, (dims, ((), ())), precision=precision, preferred_element_type=F32)


def remote(src, dst, send, recv, ctx, ten):
    return pltpu.make_async_remote_copy(
        src_ref=src, dst_ref=dst, send_sem=send, recv_sem=recv,
        device_id=(ctx, ten), device_id_type=MESH,
    )


def kernel(
    lay_h, vp_h, taps_h, pre_h, sin_h, sout_h, step_h, ld_h, skip_h, go_h,
    gi_ref, gv_ref,
    lay, vp, taps, pre, sin, sout, step, ld, skip, go,
    cum, a_ref, b_ref, gc, gp, bs1, clos, lt,
    s_send, s_recv, later, z_send, z_recv, rsuf, lsuf, y_send, y_recv, c_send, c_recv, m_send, carry,
    xo_send, xo_recv, xd_send, xd_recv, xf_send, xf_recv, x_keep, x_own,
    layh, lth, ltm, lthm, gpm, gpe, hb, w_own, v_send, v_recv, u_own, u_send, u_recv, zf_send, zf_recv, zf_own, yf_send, yf_recv,
    in_sem, lay_ss, lay_rs, s_ss, s_rs, z_ss, z_rs, y_ss, y_rs, c_ss, c_rs, m_ss, m_rs, h_ss, h_rs,
    xo_ss, xo_rs, xd_ss, xd_rs, lt_ss, lt_rs, g_ss, g_rs, v_ss, v_rs, u_ss, u_rs, zf_ss, zf_rs, yf_ss, yf_rs, lh_ss, lh_rs, xf_ss, xf_rs,
):
    c = lax.axis_index("context")
    t = lax.axis_index("tensor")
    core = lax.rem(c, NC)
    other = 1 - core
    z = lax.rem(c // NC, NZ)
    y = c // NROW
    row0 = y * NROW + core
    nxt, prv = lax.rem(c + 1, NCTX), lax.rem(c + NCTX - 1, NCTX)
    mate = c + 1 - 2 * core
    xs = [lax.rem(t + k, NX) for k in range(NX)]
    ys = [lax.rem(y + k, NY) for k in range(NY)]
    yc = [lax.rem(c + k * NROW, NCTX) for k in range(NY)]
    zs = [lax.rem(z + k, NZ) for k in range(NZ)]
    zc = [row0 + k * NC for k in zs]

    def slab(k, n):
        return pl.ds(pl.multiple_of(k * n, n), n)

    loads = {}

    def load(name, src, dst):
        loads[name] = pltpu.make_async_copy(src, dst, in_sem.at[len(loads)])
        loads[name].start()

    load("ld", ld_h, ld)
    load("go", go_h, go)
    load("sout", sout_h, sout)

    barrier = pltpu.get_barrier_semaphore()
    partners = [(zc[k], t) for k in range(1, NZ)] + [(yc[k], t) for k in range(1, NY)]
    partners += [(c, xs[1]), (c, xs[2]), (c, xs[3]), (nxt, t), (prv, t)]
    for ctx, ten in partners:
        pl.semaphore_signal(barrier, inc=1, device_id=(ctx, ten), device_id_type=MESH)

    load("sin", sin_h, sin)
    load("step", step_h, step)
    load("skip", skip_h, skip)
    load("pre", pre_h, pre)
    load("taps", taps_h, taps)
    load("vp", vp_h, vp)
    load("lay", lay_h, lay.at[t])

    def pieces(v):
        parts = []
        for _ in range(3):
            parts.append(v.astype(BF16))
            v = v - parts[-1].astype(F32)
        return parts

    ri = lax.broadcasted_iota(jnp.int32, (BLOCK, BLOCK), 0)
    ci = lax.broadcasted_iota(jnp.int32, (BLOCK, BLOCK), 1)
    upto = jnp.where(ri <= ci, 1.0, 0.0).astype(BF16)
    hi = lax.broadcasted_iota(jnp.int32, (HEADS, CH), 0)
    li = lax.broadcasted_iota(jnp.int32, (HEADS, CH), 1)
    onehot = (li // HD == hi).astype(F32)
    hi3 = lax.broadcasted_iota(jnp.int32, (3 * HEADS, CH), 0)
    li3 = lax.broadcasted_iota(jnp.int32, (3 * HEADS, CH), 1)
    onehot3 = jnp.where(li3 // HD == lax.rem(hi3, HEADS), 1.0, 0.0).astype(BF16)
    loads["ld"].wait()
    for k in range(2):
        cols = slice(k * BLOCK, (k + 1) * BLOCK)
        sums = [dot(p, upto, ((1,), (0,))) for p in pieces(ld[:, cols])]
        cum[:, cols] = (sums[2] + sums[1]) + sums[0]
    cum3 = jnp.concatenate([p.astype(F32) for p in pieces(cum[...])], axis=0).astype(BF16)
    for k in range(2):
        rows = slice(k * BLOCK, (k + 1) * BLOCK)
        b_ref[rows, :] = dot(cum3[:, rows], onehot3, ((0,), (0,)))
    clos0 = b_ref[BLOCK - 1:BLOCK, :]
    clos1 = b_ref[2 * BLOCK - 1:2 * BLOCK, :]
    clos[0:1, :] = clos0
    clos[1:2, :] = clos1
    for k in range(NC):
        s_send[k, STATE:STATE + 8, :] = jnp.broadcast_to((clos0 + clos1)[:, k * 256:(k + 1) * 256], (8, 256))

    loads["go"].wait()
    loads["sout"].wait()
    s_copy = remote(s_send.at[other], s_recv, s_ss, s_rs, mate, t)
    for half in (other, core):
        lanes = slab(half, 256)
        states = []
        for k in range(2):
            rows = slice(k * BLOCK, (k + 1) * BLOCK)
            w = (go[rows, lanes].astype(F32) * jnp.exp(b_ref[rows, lanes])).astype(BF16)
            states.append(dot(sout[rows, :], w, ((0,), (0,))))
        bs1[:, lanes] = states[1]
        s_send[half, 0:STATE, :] = states[0] + jnp.exp(clos[0:1, lanes]) * states[1]
        if half is other:
            pl.semaphore_wait(barrier, len(partners))
            s_copy.start()

    remote(lay_h, lay.at[t], lay_ss.at[0], lay_rs.at[0], c, xs[1]).start()
    remote(lay_h, lay.at[t], lay_ss.at[1], lay_rs.at[1], c, xs[3]).start()

    def within(k):
        rows = slice(k * BLOCK, (k + 1) * BLOCK)
        scores = dot(sin[rows, :], sout[rows, :], ((1,), (1,)))
        scores = jnp.where(ci >= ri, scores, 0.0)
        low = lax.broadcasted_iota(jnp.int32, (BLOCK, 128), 1) < HD
        cum_t = cum[:, rows].T
        for pair in range(HEADS // 2):
            lanes = slice(pair * 128, pair * 128 + 128)
            g = go[rows, lanes]
            parts = []
            for h in (2 * pair, 2 * pair + 1):
                spread = cum[h:h + 1, rows] - cum_t[:, h:h + 1]
                weights = (scores * jnp.exp(jnp.minimum(spread, 0.0))).astype(BF16)
                parts.append(dot(weights, g, ((1,), (0,))))
            a_ref[rows, lanes] = jnp.where(low, parts[0], parts[1])

    loads["sin"].wait()
    within(0)

    s_copy.wait_recv()
    first = jnp.where(core == 0, s_send[core], s_recv[...])
    second = jnp.where(core == 0, s_recv[...], s_send[core])
    later[...] = second
    d_first, d_second = first[STATE:STATE + 1, :], second[STATE:STATE + 1, :]
    chip = first[0:STATE, :] + jnp.exp(d_first) * second[0:STATE, :]
    z_send[:, 0:256] = chip.astype(BF16)
    d_chip = d_first + d_second
    row = lax.broadcasted_iota(jnp.int32, (16, 128), 0)

    def packed(d):
        out = jnp.zeros((16, 128), F32)
        for n, piece in enumerate(pieces(d)):
            piece = piece.astype(F32)
            out = jnp.where(row == 2 * n, piece[:, 0:128], out)
            out = jnp.where(row == 2 * n + 1, piece[:, 128:256], out)
        return out.astype(BF16)

    def unpacked(got):
        return jnp.concatenate([got[n:n + 1, :] + got[n + 2:n + 3, :] + got[n + 4:n + 5, :] for n in range(2)], axis=1)

    extra = packed(d_chip)
    for n in range(NZ):
        z_send[n * 16:(n + 1) * 16, 256:384] = extra
    for k in (4, 3, 5, 2, 6, 1, 7):
        remote(z_send.at[slab(zs[k], 16)], z_recv.at[z], z_ss, z_rs, zc[k], t).start()
    z_recv[z] = z_send[slab(z, 16), :]

    within(1)

    remote(z_send.at[pl.ds(0, 112)], z_recv.at[pl.ds(0, NZ - 1)], z_ss, z_rs, c, t).wait_recv()
    spans = [unpacked(z_recv[j][:, 256:384].astype(F32)) for j in range(NZ)]
    decays = [jnp.exp(d) for d in spans]
    r = jnp.zeros((16, 256), F32)
    for j in range(NZ - 1, -1, -1):
        rsuf[j] = r
        r = z_recv[j][:, 0:256].astype(F32) + decays[j] * r
    y_send[:, 0:256] = r.astype(BF16)
    y_send[:, 256:384] = packed(sum(spans[1:], spans[0]))
    for k in (2, 1, 3):
        remote(y_send, y_recv.at[y], y_ss, y_rs, yc[k], t).start()
    y_recv[y] = y_send[...]
    l = jnp.zeros((1, 256), F32)
    for j in range(NZ - 1, -1, -1):
        lsuf[j] = jnp.exp(l)
        l = l + spans[j]

    for k, n in ((3, 0), (1, 1)):
        remote(lay_h, lay.at[xs[k]], lay_ss.at[n], lay_rs.at[n], c, t).wait_recv()
        half = pl.ds(n * 256, 256)
        block = lay.at[xs[k], half]
        remote(block, block, lay_ss.at[2 + n], lay_rs.at[2 + n], c, xs[4 - k]).start()

    for name in ("step", "skip", "pre"):
        loads[name].wait()
    skip_e = dot(skip[...], onehot, ((1,), (0,)), HIGH)

    def factors(n):
        rows = slice(n * 64, (n + 1) * 64)
        close = clos[n // 4:n // 4 + 1, :]
        v = pre[rows, :].astype(F32)
        sig = 1.0 / (1.0 + jnp.exp(-v))
        slope = sig * (1.0 + v * (1.0 - sig))
        step_e = dot(step[:, rows], onehot, ((0,), (0,)), HIGH)
        a_ref[rows, :] = (step_e * a_ref[rows, :] + skip_e * go[rows, :].astype(F32)) * slope
        b_ref[rows, :] = step_e * jnp.exp(close - b_ref[rows, :]) * slope

    for n in range(4):
        factors(n)

    remote(y_send, y_recv.at[pl.ds(0, NY - 1)], y_ss, y_rs, c, t).wait_recv()
    coming = jnp.zeros((16, 256), F32)
    for yy in range(NY - 1, 0, -1):
        got = y_recv[yy].astype(F32)
        coming = jnp.where(yy > y, got[:, 0:256] + jnp.exp(unpacked(got[:, 256:384])) * coming, coming)
    for k in (4, 3, 5, 2, 6, 1, 7, 0):
        c_send[slab(zs[k], 16), :] = (rsuf[zs[k]] + lsuf[zs[k]] * coming).astype(BF16)
        if k:
            remote(c_send.at[slab(zs[k], 16)], c_recv.at[slab(z, 16)], c_ss, c_rs, zc[k], t).start()
    c_recv[slab(z, 16), :] = c_send[slab(z, 16), :]

    for n in range(4, 8):
        factors(n)

    def transposed(x):
        for half in range(2):
            cols = slice(half * 256, half * 256 + 256)
            tr = lay[x, cols, :].T
            for zz in range(NZ):
                for cc in range(NC):
                    f0 = (zz * NC + cc) * 16
                    lt[cc, pl.ds(pl.multiple_of(x * 128 + zz * 16, 16), 16), cols] = tr[f0:f0 + 16, :]

    loads["lay"].wait()
    for k in (0, 1, 3):
        transposed(xs[k])
    for n, rows in ((0, pl.ds(0, 256)), (1, pl.ds(256, 256))):
        block = lay.at[xs[2], rows]
        remote(block, block, lay_ss.at[2 + n], lay_rs.at[2 + n], c, t).wait_recv()
    transposed(xs[2])
    lh_copy = remote(lay.at[pl.ds(0, NX), pl.ds(ROWS - 16, 16)], layh, lh_ss, lh_rs, nxt, t)
    lh_copy.start()
    lt_copy = remote(lt.at[other], ltm, lt_ss.at[0], lt_rs.at[0], mate, t)
    lt_copy.start()
    gp[ROWS:ROWS + 128, :] = jnp.zeros((128, CH), BF16)
    gpm[ROWS + 16:ROWS + 128, :] = jnp.zeros((112, CH), BF16)
    gc[ROWS:ROWS + 8, :] = jnp.zeros((8, CH), F32)
    for name in ("taps", "vp"):
        loads[name].wait()
    decay_second = jnp.exp(later[STATE:STATE + 1, :])

    remote(c_send, c_recv.at[pl.ds(0, 112)], c_ss, c_rs, c, t).wait_recv()
    into_second = c_recv[...]
    into_first = (later[0:STATE, :] + decay_second * into_second.astype(F32)).astype(BF16)
    m_send[...] = jnp.where(core == 0, into_second, into_first)
    m_copy = remote(m_send, carry.at[core], m_ss, m_rs, mate, t)
    m_copy.start()
    carry[core] = jnp.where(core == 0, into_first, into_second)

    halo = remote(gc.at[pl.ds(0, 8)], hb, h_ss, h_rs, prv, t)

    def conv_grad(rows, lanes, carried):
        value = a_ref[rows, lanes] + b_ref[rows, lanes] * dot(sin[rows, :], carried, ((1,), (0,)))
        gc[rows, lanes] = value.astype(BF16).astype(F32)

    for half in (core, other):
        lanes = slab(half, 256)
        if half is other:
            lh_copy.wait_recv()
            for x in range(NX):
                tr = jnp.concatenate([layh[x], jnp.zeros((112, FEAT), BF16)], axis=0).T
                for zz in range(NZ):
                    for cc in range(NC):
                        f0 = (zz * NC + cc) * 16
                        lth[cc, x * 128 + zz * 16:x * 128 + zz * 16 + 16, :] = tr[f0:f0 + 16, :]
            lth_copy = remote(lth.at[other], lthm, lt_ss.at[1], lt_rs.at[1], mate, t)
            lth_copy.start()
            remote(m_send, carry.at[other], m_ss, m_rs, mate, t).wait_recv()
        into_last = carry[half]
        into_block = (bs1[:, lanes] + jnp.exp(clos[1:2, lanes]) * into_last.astype(F32)).astype(BF16)
        conv_grad(slice(0, 16), lanes, into_block)
        if half is other:
            halo.start()
        conv_grad(slice(16, TILE), lanes, into_block)
        for n in range(1, NT if half is core else NT - 1):
            conv_grad(slice(n * TILE, (n + 1) * TILE), lanes, into_block if n < NT // 2 else into_last)

    def weights_of(k):
        return vp[slab(xs[k], FEAT), :]

    def proj_grad(r0, count):
        summed = taps[0:1, :] * gc[r0 + 3:r0 + 3 + count, :]
        for j in range(1, 4):
            summed = summed + taps[j:j + 1, :] * gc[r0 + 3 - j:r0 + 3 - j + count, :]
        return summed.astype(BF16)

    def g_copy(n):
        rows = (pl.ds(0, 256), pl.ds(256, 272))[n]
        return remote(gp.at[rows], gpm.at[rows], g_ss.at[n], g_rs.at[n], mate, t)

    def piece_of(n, k):
        r0, count = PIECES[n]
        grad = gpe[...] if n == 2 else gp[r0:r0 + count, :]
        return dot(grad, weights_of(k), ((1,), (1,)))

    def xo_copy(n, s):
        rows = pl.ds(*PIECES[n])
        return remote(xo_send.at[s, rows], xo_recv.at[s, rows], xo_ss, xo_rs.at[n, s], c, xs[(1, 3)[s]])

    def xd_copy(n, s, half):
        rows = pl.ds(*PIECES[n])
        return remote(xd_send.at[s, half, rows], xd_recv.at[s, half, rows], xd_ss, xd_rs.at[n, s, half], c, xs[(1, 3)[s]])

    def far_start(n):
        rows = slice(PIECES[n][0], sum(PIECES[n]))
        part = piece_of(n, 2)
        for s in range(2):
            xo_send[s, rows, :] = part[:, s * HALF:(s + 1) * HALF].astype(BF16)
            xo_copy(n, s).start()

    def near_start(n):
        rows = slice(PIECES[n][0], sum(PIECES[n]))
        for s in range(2):
            part = piece_of(n, (1, 3)[s])
            xd_send[s, 1 - s, rows, :] = part[:, (1 - s) * HALF:(2 - s) * HALF].astype(BF16)
            xd_copy(n, s, 1 - s).start()
            x_keep[s, rows, :] = part[:, s * HALF:(s + 1) * HALF]

    def relay(n):
        rows = slice(PIECES[n][0], sum(PIECES[n]))
        for s in range(2):
            xo_copy(n, s).wait_recv()
            xd_send[s, s, rows, :] = (x_keep[s, rows, :] + xo_recv[s, rows, :].astype(F32)).astype(BF16)
            xd_copy(n, s, s).start()

    for n in range(NT):
        gp[n * TILE:(n + 1) * TILE, :] = proj_grad(n * TILE, TILE)
        if n == 1:
            g_copy(0).start()
            far_start(0)
            conv_grad(slice((NT - 1) * TILE, ROWS), slab(other, 256), into_last)

    row = lax.broadcasted_iota(jnp.int32, (16, CH), 0)
    taps_now = [taps[j:j + 1, :] for j in range(3)]
    head = [gc[j:j + 1, :] for j in range(3)]
    ahead = jnp.zeros((16, CH), F32)
    for n in range(3):
        ahead = jnp.where(row == 13 + n, sum(taps_now[j] * head[n - j] for j in range(n + 1)), ahead)
    gp[ROWS:ROWS + 16, :] = jnp.where(c == 0, 0.0, ahead).astype(BF16)
    g_copy(1).start()

    for h in range(2):
        lanes = slice(h * 256, (h + 1) * 256)
        part = dot(lt[core], gp[0:ROWS, lanes], ((1,), (0,))) + dot(lth[core], gp[ROWS:ROWS + 128, lanes], ((1,), (0,)))
        for q in (2 * h, 2 * h + 1):
            w_own[q] = part[:, (q % 2) * QW:(q % 2 + 1) * QW]

    far_start(1)

    lt_copy.wait_recv()
    lth_copy.wait_recv()
    for n in range(2):
        g_copy(n).wait_recv()
    for h in range(2):
        lanes = slice(h * 256, (h + 1) * 256)
        part = dot(ltm[...], gpm[0:ROWS, lanes], ((1,), (0,))) + dot(lthm[...], gpm[ROWS:ROWS + 128, lanes], ((1,), (0,)))
        for q in (2 * h, 2 * h + 1):
            total = w_own[q] + part[:, (q % 2) * QW:(q % 2 + 1) * QW]
            w_own[q] = total
            total = total.astype(BF16)
            if q == ZFIRST:
                for zz in range(NZ):
                    for yy in range(NY):
                        r0 = yy * 128 + zz * 16
                        zf_send[zz, yy * 16:(yy + 1) * 16, :] = total[r0:r0 + 16, :]
                for k in (4, 3, 5, 2, 6, 1, 7):
                    remote(zf_send.at[zs[k]], zf_recv.at[z], zf_ss, zf_rs, zc[k], t).start()
            else:
                for yy in range(NY):
                    v_send[q, yy] = total[yy * 128:(yy + 1) * 128, :]
                for k in (2, 1, 3):
                    remote(v_send.at[q, ys[k]], v_recv.at[q, y], v_ss.at[q], v_rs.at[q], yc[k], t).start()

    near_start(0)
    near_start(1)

    halo.wait_recv()
    gc[ROWS:ROWS + 8, :] = jnp.where(c == NCTX - 1, 0.0, hb[...])
    gpe[...] = proj_grad(ROWS - 16, 16)
    xf_send[...] = piece_of(2, 2).astype(BF16)
    xf_copy = remote(xf_send, xf_recv, xf_ss, xf_rs, c, xs[2])
    xf_copy.start()
    last = slice(PIECES[2][0], ROWS)
    for s in range(2):
        part = piece_of(2, (1, 3)[s]).astype(BF16)
        for half in range(2):
            xd_send[s, half, last, :] = part[:, half * HALF:(half + 1) * HALF]
            xd_copy(2, s, half).start()
    for n in range(3):
        x_own[PIECES[n][0]:sum(PIECES[n]), :] = piece_of(n, 0)

    def to_z(q):
        remote(v_send.at[q, pl.ds(0, NY - 1)], v_recv.at[q, pl.ds(0, NY - 1)], v_ss.at[q], v_rs.at[q], c, t).wait_recv()
        acc = w_own[q, slab(y, 128), :]
        for k in range(1, NY):
            acc = acc + v_recv[q, ys[k]].astype(F32)
        u_own[q] = acc
        u_send[q] = acc.astype(BF16)
        for k in (4, 3, 5, 2, 6, 1, 7):
            remote(u_send.at[q, slab(zs[k], 16)], u_recv.at[q, z], u_ss.at[q], u_rs.at[q], zc[k], t).start()

    def to_y():
        remote(zf_send.at[pl.ds(0, NZ - 1)], zf_recv.at[pl.ds(0, NZ - 1)], zf_ss, zf_rs, c, t).wait_recv()
        acc = jnp.concatenate([w_own[ZFIRST, pl.ds(pl.multiple_of(yy * 128 + z * 16, 16), 16), :] for yy in range(NY)], axis=0)
        for k in range(1, NZ):
            acc = acc + zf_recv[zs[k]].astype(F32)
        zf_own[...] = acc
        yf_send[...] = acc.astype(BF16)
        for k in (2, 1, 3):
            remote(yf_send.at[slab(ys[k], 16)], yf_recv.at[y], yf_ss, yf_rs, yc[k], t).start()

    relay(0)
    relay(1)
    to_z(0)
    to_z(1)
    to_y()
    to_z(2)

    for n in range(3):
        rows = slice(PIECES[n][0], sum(PIECES[n]))
        for half in range(2):
            lanes = slice(half * HALF, (half + 1) * HALF)
            acc = x_own[rows, lanes]
            if n == 2:
                if half == 0:
                    xf_copy.wait_recv()
                acc = acc + xf_recv[:, lanes].astype(F32)
            for s in range(2):
                xd_copy(n, s, half).wait_recv()
                acc = acc + xd_recv[s, half, rows, :].astype(F32)
            gi_ref[rows, lanes] = acc.astype(BF16)

    scale = 1.0 / math.sqrt(ROWS * NCTX)
    for q in (0, 1, ZFIRST, 2):
        if q == ZFIRST:
            remote(yf_send.at[pl.ds(0, 48)], yf_recv.at[pl.ds(0, NY - 1)], yf_ss, yf_rs, c, t).wait_recv()
            acc = zf_own[slab(y, 16), :]
            for k in range(1, NY):
                acc = acc + yf_recv[ys[k]].astype(F32)
        else:
            remote(u_send.at[q, pl.ds(0, 112)], u_recv.at[q, pl.ds(0, NZ - 1)], u_ss.at[q], u_rs.at[q], c, t).wait_recv()
            acc = u_own[q, slab(z, 16), :]
            for k in range(1, NZ):
                acc = acc + u_recv[q, zs[k]].astype(F32)
        gv_ref[:, q * QW:(q + 1) * QW] = acc * scale

    def sent(src, sem):
        remote(src, src, sem, h_rs, c, t).wait_send()

    sent(s_send.at[other], s_ss)
    sent(lay_h, lay_ss.at[0])
    sent(lay_h, lay_ss.at[1])
    sent(lay.at[0, pl.ds(0, 256)], lay_ss.at[2])
    sent(lay.at[0, pl.ds(0, 256)], lay_ss.at[3])
    sent(z_send.at[pl.ds(0, 112)], z_ss)
    sent(y_recv.at[pl.ds(0, NY - 1)], y_ss)
    sent(c_send.at[pl.ds(0, 112)], c_ss)
    sent(m_send, m_ss)
    sent(gc.at[pl.ds(0, 8)], h_ss)
    sent(xo_send.at[pl.ds(0, 2), pl.ds(0, PIECES[2][0])], xo_ss)
    xf_copy.wait_send()
    sent(xd_send, xd_ss)
    for q in range(Q):
        if q != ZFIRST:
            sent(v_send.at[q, pl.ds(0, NY - 1)], v_ss.at[q])
            sent(u_send.at[q, pl.ds(0, 112)], u_ss.at[q])
    sent(layh, lh_ss)
    lt_copy.wait_send()
    lth_copy.wait_send()
    for n in range(2):
        g_copy(n).wait_send()
    sent(zf_send.at[pl.ds(0, NZ - 1)], zf_ss)
    sent(yf_send.at[pl.ds(0, 48)], yf_ss)


def local(layer_input, value_proj, conv_taps, conv_pre, state_in, state_out, step_size, log_decay, skip_gain, grad_out):
    dma = pltpu.SemaphoreType.DMA
    V = pltpu.VMEM
    scratch = [
        V((NX, ROWS, FEAT), BF16), V((NX * FEAT, CH), BF16), V((4, CH), F32), V((ROWS, CH), BF16),
        V((ROWS, STATE), BF16), V((ROWS, STATE), BF16), V((HEADS, ROWS), F32), V((HEADS, ROWS), F32),
        V((1, HEADS), F32), V((ROWS, CH), BF16),
        V((HEADS, ROWS), F32), V((ROWS, CH), F32), V((ROWS, CH), F32), V((ROWS + 8, CH), F32), V((ROWS + 128, CH), BF16),
        V((STATE, CH), F32), V((8, CH), F32), V((NC, ROWS, ROWS), BF16),
        V((NC, STATE + 8, 256), F32), V((STATE + 8, 256), F32), V((STATE + 8, 256), F32),
        V((STATE, 384), BF16), V((NZ, 16, 384), BF16), V((NZ, 16, 256), F32), V((NZ, 1, 256), F32),
        V((16, 384), BF16), V((NY, 16, 384), BF16),
        V((STATE, 256), BF16), V((STATE, 256), BF16), V((STATE, 256), BF16), V((NC, STATE, 256), BF16),
        V((2, ROWS, HALF), BF16), V((2, ROWS, HALF), BF16), V((2, 2, ROWS, HALF), BF16), V((2, 2, ROWS, HALF), BF16),
        V((16, FEAT), BF16), V((16, FEAT), BF16), V((2, ROWS, HALF), F32), V((ROWS, FEAT), F32),
        V((NX, 16, FEAT), BF16), V((NC, 512, 128), BF16), V((512, ROWS), BF16), V((512, 128), BF16), V((ROWS + 128, CH), BF16),
        V((16, CH), BF16), V((8, CH), F32), V((Q, 512, QW), F32),
        V((Q, NY, 128, QW), BF16), V((Q, NY, 128, QW), BF16), V((Q, 128, QW), F32), V((Q, 128, QW), BF16), V((Q, NZ, 16, QW), BF16),
        V((NZ, 64, QW), BF16), V((NZ, 64, QW), BF16), V((64, QW), F32), V((64, QW), BF16), V((NY, 16, QW), BF16),
        dma((10,)), dma((4,)), dma((4,)), dma, dma, dma, dma, dma, dma, dma, dma, dma, dma, dma, dma,
        dma, dma((3, 2)), dma, dma((3, 2, 2)), dma((2,)), dma((2,)), dma((2,)), dma((2,)), dma((Q,)), dma((Q,)), dma((Q,)), dma((Q,)), dma, dma, dma, dma, dma, dma,
        dma, dma,
    ]
    outs = (V((ROWS, FEAT), BF16), V((16, CH), F32))
    return pl.pallas_call(
        kernel,
        out_shape=outs,
        in_specs=[pl.BlockSpec(memory_space=pl.ANY)] * 10,
        out_specs=(pl.BlockSpec(memory_space=pltpu.VMEM), pl.BlockSpec(memory_space=pltpu.VMEM)),
        scratch_shapes=scratch,
        compiler_params=pltpu.CompilerParams(
            collective_id=0, has_side_effects=True, vmem_limit_bytes=60 * 2**20
        ),
        cost_estimate=pl.CostEstimate(flops=1_500_000_000, bytes_accessed=4_000_000, transcendentals=2_000_000),
        name="scan_backward",
    )(
        layer_input, value_proj, conv_taps, conv_pre, state_in, state_out, step_size, log_decay,
        skip_gain.reshape(1, HEADS), grad_out,
    )


def solution(mesh):
    return jax.shard_map(
        local,
        mesh=mesh,
        in_specs=(
            P("context", "tensor"),
            P(None, "tensor"),
            P(None, "tensor"),
            P("context", "tensor"),
            P("context", None),
            P("context", None),
            P("tensor", "context"),
            P("tensor", "context"),
            P("tensor"),
            P("context", "tensor"),
        ),
        out_specs=(P("context", "tensor"), P("context", "tensor")),
        check_vma=False,
    )
```

```python
import functools
import math

import jax
import jax.numpy as jnp
from jax import lax
from jax.experimental import pallas as pl
from jax.experimental.pallas import tpu as pltpu
from jax.sharding import PartitionSpec as P

MESH = pl.DeviceIdType.MESH
F32, BF16 = jnp.float32, jnp.bfloat16
HIGH = lax.Precision.HIGHEST

NX, NY, NZ, NC = 4, 4, 8, 2
NROW = NZ * NC
NCTX = NY * NROW
ROWS, CH, STATE, BLOCK, HEADS, HD = 512, 512, 128, 256, 8, 64
FEAT, HALF = 256, 128
Q, QW = 4, 128
ZFIRST = 3
TILE, NT = 128, 4
PIECES = ((0, 256), (256, 240), (496, 16))


def dot(a, b, dims, precision=None):
    return lax.dot_general(a, b, (dims, ((), ())), precision=precision, preferred_element_type=F32)


def remote(src, dst, send, recv, ctx, ten):
    return pltpu.make_async_remote_copy(
        src_ref=src, dst_ref=dst, send_sem=send, recv_sem=recv,
        device_id=(ctx, ten), device_id_type=MESH,
    )


def kernel(
    lay_h, vp_h, taps_h, pre_h, sin_h, sout_h, step_h, ld_h, skip_h, go_h,
    gi_ref, gv_ref,
    lay, vp, taps, pre, sin, sout, step, ld, skip, go,
    cum, a_ref, b_ref, gc, gp, bs1, clos, lt,
    s_send, s_recv, later, z_send, z_recv, rsuf, lsuf, y_send, y_recv, c_send, c_recv, m_send, carry,
    xo_send, xo_recv, xd_send, xd_recv, xf_send, xf_recv, x_keep, x_own,
    layh, lth, ltm, lthm, gpm, gpe, hb, w_own, v_send, v_recv, u_own, u_send, u_recv, zf_send, zf_recv, zf_own, yf_send, yf_recv,
    in_sem, lay_ss, lay_rs, s_ss, s_rs, z_ss, z_rs, y_ss, y_rs, c_ss, c_rs, m_ss, m_rs, h_ss, h_rs,
    xo_ss, xo_rs, xd_ss, xd_rs, lt_ss, lt_rs, g_ss, g_rs, v_ss, v_rs, u_ss, u_rs, zf_ss, zf_rs, yf_ss, yf_rs, lh_ss, lh_rs, xf_ss, xf_rs,
):
    c = lax.axis_index("context")
    t = lax.axis_index("tensor")
    core = lax.rem(c, NC)
    other = 1 - core
    z = lax.rem(c // NC, NZ)
    y = c // NROW
    row0 = y * NROW + core
    nxt, prv = lax.rem(c + 1, NCTX), lax.rem(c + NCTX - 1, NCTX)
    mate = c + 1 - 2 * core
    xs = [lax.rem(t + k, NX) for k in range(NX)]
    ys = [lax.rem(y + k, NY) for k in range(NY)]
    yc = [lax.rem(c + k * NROW, NCTX) for k in range(NY)]
    zs = [lax.rem(z + k, NZ) for k in range(NZ)]
    zc = [row0 + k * NC for k in zs]

    def slab(k, n):
        return pl.ds(pl.multiple_of(k * n, n), n)

    loads = {}

    def load(name, src, dst):
        loads[name] = pltpu.make_async_copy(src, dst, in_sem.at[len(loads)])
        loads[name].start()

    load("ld", ld_h, ld)
    load("go", go_h, go)
    load("sout", sout_h, sout)

    barrier = pltpu.get_barrier_semaphore()
    partners = [(zc[k], t) for k in range(1, NZ)] + [(yc[k], t) for k in range(1, NY)]
    partners += [(c, xs[1]), (c, xs[2]), (c, xs[3]), (nxt, t), (prv, t)]
    for ctx, ten in partners:
        pl.semaphore_signal(barrier, inc=1, device_id=(ctx, ten), device_id_type=MESH)

    load("sin", sin_h, sin)
    load("step", step_h, step)
    load("skip", skip_h, skip)
    load("pre", pre_h, pre)
    load("taps", taps_h, taps)
    load("vp", vp_h, vp)
    load("lay", lay_h, lay.at[t])

    def pieces(v):
        parts = []
        for _ in range(3):
            parts.append(v.astype(BF16))
            v = v - parts[-1].astype(F32)
        return parts

    ri = lax.broadcasted_iota(jnp.int32, (BLOCK, BLOCK), 0)
    ci = lax.broadcasted_iota(jnp.int32, (BLOCK, BLOCK), 1)
    upto = jnp.where(ri <= ci, 1.0, 0.0).astype(BF16)
    hi = lax.broadcasted_iota(jnp.int32, (HEADS, CH), 0)
    li = lax.broadcasted_iota(jnp.int32, (HEADS, CH), 1)
    onehot = (li // HD == hi).astype(F32)
    hi3 = lax.broadcasted_iota(jnp.int32, (3 * HEADS, CH), 0)
    li3 = lax.broadcasted_iota(jnp.int32, (3 * HEADS, CH), 1)
    onehot3 = jnp.where(li3 // HD == lax.rem(hi3, HEADS), 1.0, 0.0).astype(BF16)
    loads["ld"].wait()
    for k in range(2):
        cols = slice(k * BLOCK, (k + 1) * BLOCK)
        sums = [dot(p, upto, ((1,), (0,))) for p in pieces(ld[:, cols])]
        cum[:, cols] = (sums[2] + sums[1]) + sums[0]
    cum3 = jnp.concatenate([p.astype(F32) for p in pieces(cum[...])], axis=0).astype(BF16)
    for k in range(2):
        rows = slice(k * BLOCK, (k + 1) * BLOCK)
        b_ref[rows, :] = dot(cum3[:, rows], onehot3, ((0,), (0,)))
    clos0 = b_ref[BLOCK - 1:BLOCK, :]
    clos1 = b_ref[2 * BLOCK - 1:2 * BLOCK, :]
    clos[0:1, :] = clos0
    clos[1:2, :] = clos1
    for k in range(NC):
        s_send[k, STATE:STATE + 8, :] = jnp.broadcast_to((clos0 + clos1)[:, k * 256:(k + 1) * 256], (8, 256))

    loads["go"].wait()
    loads["sout"].wait()
    s_copy = remote(s_send.at[other], s_recv, s_ss, s_rs, mate, t)
    for half in (other, core):
        lanes = slab(half, 256)
        states = []
        for k in range(2):
            rows = slice(k * BLOCK, (k + 1) * BLOCK)
            w = (go[rows, lanes].astype(F32) * jnp.exp(b_ref[rows, lanes])).astype(BF16)
            states.append(dot(sout[rows, :], w, ((0,), (0,))))
        bs1[:, lanes] = states[1]
        s_send[half, 0:STATE, :] = states[0] + jnp.exp(clos[0:1, lanes]) * states[1]
        if half is other:
            pl.semaphore_wait(barrier, len(partners))
            s_copy.start()

    remote(lay_h, lay.at[t], lay_ss.at[0], lay_rs.at[0], c, xs[1]).start()
    remote(lay_h, lay.at[t], lay_ss.at[1], lay_rs.at[1], c, xs[3]).start()

    def within(k):
        rows = slice(k * BLOCK, (k + 1) * BLOCK)
        scores = dot(sin[rows, :], sout[rows, :], ((1,), (1,)))
        scores = jnp.where(ci >= ri, scores, 0.0)
        low = lax.broadcasted_iota(jnp.int32, (BLOCK, 128), 1) < HD
        cum_t = cum[:, rows].T
        for pair in range(HEADS // 2):
            lanes = slice(pair * 128, pair * 128 + 128)
            g = go[rows, lanes]
            parts = []
            for h in (2 * pair, 2 * pair + 1):
                spread = cum[h:h + 1, rows] - cum_t[:, h:h + 1]
                weights = (scores * jnp.exp(jnp.minimum(spread, 0.0))).astype(BF16)
                parts.append(dot(weights, g, ((1,), (0,))))
            a_ref[rows, lanes] = jnp.where(low, parts[0], parts[1])

    loads["sin"].wait()
    within(0)

    s_copy.wait_recv()
    first = jnp.where(core == 0, s_send[core], s_recv[...])
    second = jnp.where(core == 0, s_recv[...], s_send[core])
    later[...] = second
    d_first, d_second = first[STATE:STATE + 1, :], second[STATE:STATE + 1, :]
    chip = first[0:STATE, :] + jnp.exp(d_first) * second[0:STATE, :]
    z_send[:, 0:256] = chip.astype(BF16)
    d_chip = d_first + d_second
    row = lax.broadcasted_iota(jnp.int32, (16, 128), 0)

    def packed(d):
        out = jnp.zeros((16, 128), F32)
        for n, piece in enumerate(pieces(d)):
            piece = piece.astype(F32)
            out = jnp.where(row == 2 * n, piece[:, 0:128], out)
            out = jnp.where(row == 2 * n + 1, piece[:, 128:256], out)
        return out.astype(BF16)

    def unpacked(got):
        return jnp.concatenate([got[n:n + 1, :] + got[n + 2:n + 3, :] + got[n + 4:n + 5, :] for n in range(2)], axis=1)

    extra = packed(d_chip)
    for n in range(NZ):
        z_send[n * 16:(n + 1) * 16, 256:384] = extra
    for k in (4, 3, 5, 2, 6, 1, 7):
        remote(z_send.at[slab(zs[k], 16)], z_recv.at[z], z_ss, z_rs, zc[k], t).start()
    z_recv[z] = z_send[slab(z, 16), :]

    within(1)

    remote(z_send.at[pl.ds(0, 112)], z_recv.at[pl.ds(0, NZ - 1)], z_ss, z_rs, c, t).wait_recv()
    spans = [unpacked(z_recv[j][:, 256:384].astype(F32)) for j in range(NZ)]
    decays = [jnp.exp(d) for d in spans]
    r = jnp.zeros((16, 256), F32)
    for j in range(NZ - 1, -1, -1):
        rsuf[j] = r
        r = z_recv[j][:, 0:256].astype(F32) + decays[j] * r
    y_send[:, 0:256] = r.astype(BF16)
    y_send[:, 256:384] = packed(sum(spans[1:], spans[0]))
    for k in (2, 1, 3):
        remote(y_send, y_recv.at[y], y_ss, y_rs, yc[k], t).start()
    y_recv[y] = y_send[...]
    l = jnp.zeros((1, 256), F32)
    for j in range(NZ - 1, -1, -1):
        lsuf[j] = jnp.exp(l)
        l = l + spans[j]

    for k, n in ((3, 0), (1, 1)):
        remote(lay_h, lay.at[xs[k]], lay_ss.at[n], lay_rs.at[n], c, t).wait_recv()
        half = pl.ds(n * 256, 256)
        block = lay.at[xs[k], half]
        remote(block, block, lay_ss.at[2 + n], lay_rs.at[2 + n], c, xs[4 - k]).start()

    for name in ("step", "skip", "pre"):
        loads[name].wait()
    skip_e = dot(skip[...], onehot, ((1,), (0,)), HIGH)

    def factors(n):
        rows = slice(n * 64, (n + 1) * 64)
        close = clos[n // 4:n // 4 + 1, :]
        v = pre[rows, :].astype(F32)
        sig = 1.0 / (1.0 + jnp.exp(-v))
        slope = sig * (1.0 + v * (1.0 - sig))
        step_e = dot(step[:, rows], onehot, ((0,), (0,)), HIGH)
        a_ref[rows, :] = (step_e * a_ref[rows, :] + skip_e * go[rows, :].astype(F32)) * slope
        b_ref[rows, :] = step_e * jnp.exp(close - b_ref[rows, :]) * slope

    for n in range(4):
        factors(n)

    remote(y_send, y_recv.at[pl.ds(0, NY - 1)], y_ss, y_rs, c, t).wait_recv()
    coming = jnp.zeros((16, 256), F32)
    for yy in range(NY - 1, 0, -1):
        got = y_recv[yy].astype(F32)
        coming = jnp.where(yy > y, got[:, 0:256] + jnp.exp(unpacked(got[:, 256:384])) * coming, coming)
    for k in (4, 3, 5, 2, 6, 1, 7, 0):
        c_send[slab(zs[k], 16), :] = (rsuf[zs[k]] + lsuf[zs[k]] * coming).astype(BF16)
        if k:
            remote(c_send.at[slab(zs[k], 16)], c_recv.at[slab(z, 16)], c_ss, c_rs, zc[k], t).start()
    c_recv[slab(z, 16), :] = c_send[slab(z, 16), :]

    for n in range(4, 8):
        factors(n)

    def transposed(x):
        for half in range(2):
            cols = slice(half * 256, half * 256 + 256)
            tr = lay[x, cols, :].T
            for zz in range(NZ):
                for cc in range(NC):
                    f0 = (zz * NC + cc) * 16
                    lt[cc, pl.ds(pl.multiple_of(x * 128 + zz * 16, 16), 16), cols] = tr[f0:f0 + 16, :]

    loads["lay"].wait()
    for k in (0, 1, 3):
        transposed(xs[k])
    for n, rows in ((0, pl.ds(0, 256)), (1, pl.ds(256, 256))):
        block = lay.at[xs[2], rows]
        remote(block, block, lay_ss.at[2 + n], lay_rs.at[2 + n], c, t).wait_recv()
    transposed(xs[2])
    lh_copy = remote(lay.at[pl.ds(0, NX), pl.ds(ROWS - 16, 16)], layh, lh_ss, lh_rs, nxt, t)
    lh_copy.start()
    lt_copy = remote(lt.at[other], ltm, lt_ss.at[0], lt_rs.at[0], mate, t)
    lt_copy.start()
    gp[ROWS:ROWS + 128, :] = jnp.zeros((128, CH), BF16)
    gpm[ROWS + 16:ROWS + 128, :] = jnp.zeros((112, CH), BF16)
    gc[ROWS:ROWS + 8, :] = jnp.zeros((8, CH), F32)
    for name in ("taps", "vp"):
        loads[name].wait()
    decay_second = jnp.exp(later[STATE:STATE + 1, :])

    remote(c_send, c_recv.at[pl.ds(0, 112)], c_ss, c_rs, c, t).wait_recv()
    into_second = c_recv[...]
    into_first = (later[0:STATE, :] + decay_second * into_second.astype(F32)).astype(BF16)
    m_send[...] = jnp.where(core == 0, into_second, into_first)
    m_copy = remote(m_send, carry.at[core], m_ss, m_rs, mate, t)
    m_copy.start()
    carry[core] = jnp.where(core == 0, into_first, into_second)

    halo = remote(gc.at[pl.ds(0, 8)], hb, h_ss, h_rs, prv, t)

    def conv_grad(rows, lanes, carried):
        value = a_ref[rows, lanes] + b_ref[rows, lanes] * dot(sin[rows, :], carried, ((1,), (0,)))
        gc[rows, lanes] = value.astype(BF16).astype(F32)

    for half in (core, other):
        lanes = slab(half, 256)
        if half is other:
            lh_copy.wait_recv()
            for x in range(NX):
                tr = jnp.concatenate([layh[x], jnp.zeros((112, FEAT), BF16)], axis=0).T
                for zz in range(NZ):
                    for cc in range(NC):
                        f0 = (zz * NC + cc) * 16
                        lth[cc, x * 128 + zz * 16:x * 128 + zz * 16 + 16, :] = tr[f0:f0 + 16, :]
            lth_copy = remote(lth.at[other], lthm, lt_ss.at[1], lt_rs.at[1], mate, t)
            lth_copy.start()
            remote(m_send, carry.at[other], m_ss, m_rs, mate, t).wait_recv()
        into_last = carry[half]
        into_block = (bs1[:, lanes] + jnp.exp(clos[1:2, lanes]) * into_last.astype(F32)).astype(BF16)
        conv_grad(slice(0, 16), lanes, into_block)
        if half is other:
            halo.start()
        conv_grad(slice(16, TILE), lanes, into_block)
        for n in range(1, NT if half is core else NT - 1):
            conv_grad(slice(n * TILE, (n + 1) * TILE), lanes, into_block if n < NT // 2 else into_last)

    def weights_of(k):
        return vp[slab(xs[k], FEAT), :]

    def proj_grad(r0, count):
        summed = taps[0:1, :] * gc[r0 + 3:r0 + 3 + count, :]
        for j in range(1, 4):
            summed = summed + taps[j:j + 1, :] * gc[r0 + 3 - j:r0 + 3 - j + count, :]
        return summed.astype(BF16)

    def g_copy(n):
        rows = (pl.ds(0, 256), pl.ds(256, 272))[n]
        return remote(gp.at[rows], gpm.at[rows], g_ss.at[n], g_rs.at[n], mate, t)

    def piece_of(n, k):
        r0, count = PIECES[n]
        grad = gpe[...] if n == 2 else gp[r0:r0 + count, :]
        return dot(grad, weights_of(k), ((1,), (1,)))

    def xo_copy(n, s):
        rows = pl.ds(*PIECES[n])
        return remote(xo_send.at[s, rows], xo_recv.at[s, rows], xo_ss, xo_rs.at[n, s], c, xs[(1, 3)[s]])

    def xd_copy(n, s, half):
        rows = pl.ds(*PIECES[n])
        return remote(xd_send.at[s, half, rows], xd_recv.at[s, half, rows], xd_ss, xd_rs.at[n, s, half], c, xs[(1, 3)[s]])

    def far_start(n):
        rows = slice(PIECES[n][0], sum(PIECES[n]))
        part = piece_of(n, 2)
        for s in range(2):
            xo_send[s, rows, :] = part[:, s * HALF:(s + 1) * HALF].astype(BF16)
            xo_copy(n, s).start()

    def near_start(n):
        rows = slice(PIECES[n][0], sum(PIECES[n]))
        for s in range(2):
            part = piece_of(n, (1, 3)[s])
            xd_send[s, 1 - s, rows, :] = part[:, (1 - s) * HALF:(2 - s) * HALF].astype(BF16)
            xd_copy(n, s, 1 - s).start()
            x_keep[s, rows, :] = part[:, s * HALF:(s + 1) * HALF]

    def relay(n):
        rows = slice(PIECES[n][0], sum(PIECES[n]))
        for s in range(2):
            xo_copy(n, s).wait_recv()
            xd_send[s, s, rows, :] = (x_keep[s, rows, :] + xo_recv[s, rows, :].astype(F32)).astype(BF16)
            xd_copy(n, s, s).start()

    for n in range(NT):
        gp[n * TILE:(n + 1) * TILE, :] = proj_grad(n * TILE, TILE)
        if n == 1:
            g_copy(0).start()
            far_start(0)
            conv_grad(slice((NT - 1) * TILE, ROWS), slab(other, 256), into_last)

    row = lax.broadcasted_iota(jnp.int32, (16, CH), 0)
    taps_now = [taps[j:j + 1, :] for j in range(3)]
    head = [gc[j:j + 1, :] for j in range(3)]
    ahead = jnp.zeros((16, CH), F32)
    for n in range(3):
        ahead = jnp.where(row == 13 + n, sum(taps_now[j] * head[n - j] for j in range(n + 1)), ahead)
    gp[ROWS:ROWS + 16, :] = jnp.where(c == 0, 0.0, ahead).astype(BF16)
    g_copy(1).start()

    for h in range(2):
        lanes = slice(h * 256, (h + 1) * 256)
        part = dot(lt[core], gp[0:ROWS, lanes], ((1,), (0,))) + dot(lth[core], gp[ROWS:ROWS + 128, lanes], ((1,), (0,)))
        for q in (2 * h, 2 * h + 1):
            w_own[q] = part[:, (q % 2) * QW:(q % 2 + 1) * QW]

    far_start(1)

    lt_copy.wait_recv()
    lth_copy.wait_recv()
    for n in range(2):
        g_copy(n).wait_recv()
    for h in range(2):
        lanes = slice(h * 256, (h + 1) * 256)
        part = dot(ltm[...], gpm[0:ROWS, lanes], ((1,), (0,))) + dot(lthm[...], gpm[ROWS:ROWS + 128, lanes], ((1,), (0,)))
        for q in (2 * h, 2 * h + 1):
            total = w_own[q] + part[:, (q % 2) * QW:(q % 2 + 1) * QW]
            w_own[q] = total
            total = total.astype(BF16)
            if q == ZFIRST:
                for zz in range(NZ):
                    for yy in range(NY):
                        r0 = yy * 128 + zz * 16
                        zf_send[zz, yy * 16:(yy + 1) * 16, :] = total[r0:r0 + 16, :]
                for k in (4, 3, 5, 2, 6, 1, 7):
                    remote(zf_send.at[zs[k]], zf_recv.at[z], zf_ss, zf_rs, zc[k], t).start()
            else:
                for yy in range(NY):
                    v_send[q, yy] = total[yy * 128:(yy + 1) * 128, :]
                for k in (2, 1, 3):
                    remote(v_send.at[q, ys[k]], v_recv.at[q, y], v_ss.at[q], v_rs.at[q], yc[k], t).start()

    near_start(0)
    near_start(1)

    halo.wait_recv()
    gc[ROWS:ROWS + 8, :] = jnp.where(c == NCTX - 1, 0.0, hb[...])
    gpe[...] = proj_grad(ROWS - 16, 16)
    xf_send[...] = piece_of(2, 2).astype(BF16)
    xf_copy = remote(xf_send, xf_recv, xf_ss, xf_rs, c, xs[2])
    xf_copy.start()
    last = slice(PIECES[2][0], ROWS)
    for s in range(2):
        part = piece_of(2, (1, 3)[s]).astype(BF16)
        for half in range(2):
            xd_send[s, half, last, :] = part[:, half * HALF:(half + 1) * HALF]
            xd_copy(2, s, half).start()
    for n in range(3):
        x_own[PIECES[n][0]:sum(PIECES[n]), :] = piece_of(n, 0)

    def to_z(q):
        remote(v_send.at[q, pl.ds(0, NY - 1)], v_recv.at[q, pl.ds(0, NY - 1)], v_ss.at[q], v_rs.at[q], c, t).wait_recv()
        acc = w_own[q, slab(y, 128), :]
        for k in range(1, NY):
            acc = acc + v_recv[q, ys[k]].astype(F32)
        u_own[q] = acc
        u_send[q] = acc.astype(BF16)
        for k in (4, 3, 5, 2, 6, 1, 7):
            remote(u_send.at[q, slab(zs[k], 16)], u_recv.at[q, z], u_ss.at[q], u_rs.at[q], zc[k], t).start()

    def to_y():
        remote(zf_send.at[pl.ds(0, NZ - 1)], zf_recv.at[pl.ds(0, NZ - 1)], zf_ss, zf_rs, c, t).wait_recv()
        acc = jnp.concatenate([w_own[ZFIRST, pl.ds(pl.multiple_of(yy * 128 + z * 16, 16), 16), :] for yy in range(NY)], axis=0)
        for k in range(1, NZ):
            acc = acc + zf_recv[zs[k]].astype(F32)
        zf_own[...] = acc
        yf_send[...] = acc.astype(BF16)
        for k in (2, 1, 3):
            remote(yf_send.at[slab(ys[k], 16)], yf_recv.at[y], yf_ss, yf_rs, yc[k], t).start()

    relay(0)
    to_z(0)
    relay(1)
    to_z(1)
    to_y()
    to_z(2)

    for n in range(3):
        rows = slice(PIECES[n][0], sum(PIECES[n]))
        for half in range(2):
            lanes = slice(half * HALF, (half + 1) * HALF)
            acc = x_own[rows, lanes]
            if n == 2:
                if half == 0:
                    xf_copy.wait_recv()
                acc = acc + xf_recv[:, lanes].astype(F32)
            for s in range(2):
                xd_copy(n, s, half).wait_recv()
                acc = acc + xd_recv[s, half, rows, :].astype(F32)
            gi_ref[rows, lanes] = acc.astype(BF16)

    scale = 1.0 / math.sqrt(ROWS * NCTX)
    for q in (0, 1, ZFIRST, 2):
        if q == ZFIRST:
            remote(yf_send.at[pl.ds(0, 48)], yf_recv.at[pl.ds(0, NY - 1)], yf_ss, yf_rs, c, t).wait_recv()
            acc = zf_own[slab(y, 16), :]
            for k in range(1, NY):
                acc = acc + yf_recv[ys[k]].astype(F32)
        else:
            remote(u_send.at[q, pl.ds(0, 112)], u_recv.at[q, pl.ds(0, NZ - 1)], u_ss.at[q], u_rs.at[q], c, t).wait_recv()
            acc = u_own[q, slab(z, 16), :]
            for k in range(1, NZ):
                acc = acc + u_recv[q, zs[k]].astype(F32)
        gv_ref[:, q * QW:(q + 1) * QW] = acc * scale

    def sent(src, sem):
        remote(src, src, sem, h_rs, c, t).wait_send()

    sent(s_send.at[other], s_ss)
    sent(lay_h, lay_ss.at[0])
    sent(lay_h, lay_ss.at[1])
    sent(lay.at[0, pl.ds(0, 256)], lay_ss.at[2])
    sent(lay.at[0, pl.ds(0, 256)], lay_ss.at[3])
    sent(z_send.at[pl.ds(0, 112)], z_ss)
    sent(y_recv.at[pl.ds(0, NY - 1)], y_ss)
    sent(c_send.at[pl.ds(0, 112)], c_ss)
    sent(m_send, m_ss)
    sent(gc.at[pl.ds(0, 8)], h_ss)
    sent(xo_send.at[pl.ds(0, 2), pl.ds(0, PIECES[2][0])], xo_ss)
    xf_copy.wait_send()
    sent(xd_send, xd_ss)
    for q in range(Q):
        if q != ZFIRST:
            sent(v_send.at[q, pl.ds(0, NY - 1)], v_ss.at[q])
            sent(u_send.at[q, pl.ds(0, 112)], u_ss.at[q])
    sent(layh, lh_ss)
    lt_copy.wait_send()
    lth_copy.wait_send()
    for n in range(2):
        g_copy(n).wait_send()
    sent(zf_send.at[pl.ds(0, NZ - 1)], zf_ss)
    sent(yf_send.at[pl.ds(0, 48)], yf_ss)


def local(layer_input, value_proj, conv_taps, conv_pre, state_in, state_out, step_size, log_decay, skip_gain, grad_out):
    dma = pltpu.SemaphoreType.DMA
    V = pltpu.VMEM
    scratch = [
        V((NX, ROWS, FEAT), BF16), V((NX * FEAT, CH), BF16), V((4, CH), F32), V((ROWS, CH), BF16),
        V((ROWS, STATE), BF16), V((ROWS, STATE), BF16), V((HEADS, ROWS), F32), V((HEADS, ROWS), F32),
        V((1, HEADS), F32), V((ROWS, CH), BF16),
        V((HEADS, ROWS), F32), V((ROWS, CH), F32), V((ROWS, CH), F32), V((ROWS + 8, CH), F32), V((ROWS + 128, CH), BF16),
        V((STATE, CH), F32), V((8, CH), F32), V((NC, ROWS, ROWS), BF16),
        V((NC, STATE + 8, 256), F32), V((STATE + 8, 256), F32), V((STATE + 8, 256), F32),
        V((STATE, 384), BF16), V((NZ, 16, 384), BF16), V((NZ, 16, 256), F32), V((NZ, 1, 256), F32),
        V((16, 384), BF16), V((NY, 16, 384), BF16),
        V((STATE, 256), BF16), V((STATE, 256), BF16), V((STATE, 256), BF16), V((NC, STATE, 256), BF16),
        V((2, ROWS, HALF), BF16), V((2, ROWS, HALF), BF16), V((2, 2, ROWS, HALF), BF16), V((2, 2, ROWS, HALF), BF16),
        V((16, FEAT), BF16), V((16, FEAT), BF16), V((2, ROWS, HALF), F32), V((ROWS, FEAT), F32),
        V((NX, 16, FEAT), BF16), V((NC, 512, 128), BF16), V((512, ROWS), BF16), V((512, 128), BF16), V((ROWS + 128, CH), BF16),
        V((16, CH), BF16), V((8, CH), F32), V((Q, 512, QW), F32),
        V((Q, NY, 128, QW), BF16), V((Q, NY, 128, QW), BF16), V((Q, 128, QW), F32), V((Q, 128, QW), BF16), V((Q, NZ, 16, QW), BF16),
        V((NZ, 64, QW), BF16), V((NZ, 64, QW), BF16), V((64, QW), F32), V((64, QW), BF16), V((NY, 16, QW), BF16),
        dma((10,)), dma((4,)), dma((4,)), dma, dma, dma, dma, dma, dma, dma, dma, dma, dma, dma, dma,
        dma, dma((3, 2)), dma, dma((3, 2, 2)), dma((2,)), dma((2,)), dma((2,)), dma((2,)), dma((Q,)), dma((Q,)), dma((Q,)), dma((Q,)), dma, dma, dma, dma, dma, dma,
        dma, dma,
    ]
    outs = (V((ROWS, FEAT), BF16), V((16, CH), F32))
    return pl.pallas_call(
        kernel,
        out_shape=outs,
        in_specs=[pl.BlockSpec(memory_space=pl.ANY)] * 10,
        out_specs=(pl.BlockSpec(memory_space=pltpu.VMEM), pl.BlockSpec(memory_space=pltpu.VMEM)),
        scratch_shapes=scratch,
        compiler_params=pltpu.CompilerParams(
            collective_id=0, has_side_effects=True, vmem_limit_bytes=60 * 2**20
        ),
        cost_estimate=pl.CostEstimate(flops=1_500_000_000, bytes_accessed=4_000_000, transcendentals=2_000_000),
        name="scan_backward",
    )(
        layer_input, value_proj, conv_taps, conv_pre, state_in, state_out, step_size, log_decay,
        skip_gain.reshape(1, HEADS), grad_out,
    )


def solution(mesh):
    return jax.shard_map(
        local,
        mesh=mesh,
        in_specs=(
            P("context", "tensor"),
            P(None, "tensor"),
            P(None, "tensor"),
            P("context", "tensor"),
            P("context", None),
            P("context", None),
            P("tensor", "context"),
            P("tensor", "context"),
            P("tensor"),
            P("context", "tensor"),
        ),
        out_specs=(P("context", "tensor"), P("context", "tensor")),
        check_vma=False,
    )
```
